32 devices in a mesh: row: 8 (over z, x), col: 4 (over y, core).
Axes of the slice: x: 2, y: 2, z: 4, core: 2. Of those that a mesh axis runs over, the one named last changes fastest.
Arguments:
- front: float32 [9216, 9216], P('row', 'col')
- child_tiles: float32 [4096, 4096], P(('row', 'col')), may hold values from -0.4375 to 0.4375
- tile_target: int32 [4096], P(('row', 'col')), may hold values from 0 to 20735, as said below
- tile_count: int32 [128], P(('row', 'col')), may hold values from 24 to 32
- probe: float32 [9216, 512], P('col'), may hold values from -1.75 to 1.75
Outputs:
- panel_factor: float32 [9216, 1024], P('row', 'col')
- sketch: float32 [9216, 512], P('row', 'col')
The draws below stay inside these ranges and needn't reach their ends.
Inputs may be any that keep to these rules, and one draw needn't show every extreme that they name: `tile_target`: among the 128 slots of one device, live or not, each counted once at its target tile and once at the mirrored tile, at most 8 placements fall inside the block of the front held by any one device.
All inputs are finite; a program needn't handle non-finite values.
Results may differ from the reference program's by a relative error of at most 0.00015.
Values sent between devices are 32-bit elements; how exact they have to be, the bound alone decides.
No kernel may reach another device: no remote copies, remote signals or barrier semaphores. Data moves between devices by JAX's collectives and lax.ppermute only.
A program may use at most 128 MiB of HBM per device.

```python
import math
import jax
import jax.numpy as jnp
from jax import lax

F = 9216
NB = 512
PANELS = 2
SK = 512
TB = 64
CHILDREN = 4
SLOTS = 32
CAP = 8
N_ROW = 8
N_COL = 4
DEVICES = 32


def draw_front(key, part):
    first, second, scale_key = jax.random.split(jax.random.fold_in(key, 11), 3)
    noise = jax.random.normal(first, (F, F), jnp.float32)
    symmetric = (noise + noise.T) * (3.0 / math.sqrt(2.0 * F))
    scales = jax.random.uniform(scale_key, (F,), jnp.float32, 1.2, 2.4)
    positions = jnp.arange(F, dtype=jnp.float32)
    offsets = positions[:, None] - positions[None, :]
    kernel = scales[:, None] * scales[None, :] * jnp.exp(offsets * offsets * (-0.5 / 1600.0))
    diagonal = jax.random.uniform(second, (F,), jnp.float32, 14.0, 28.0)
    spots = jnp.arange(F)
    return (symmetric + kernel).at[spots, spots].add(diagonal)


def draw_tile_target(key, part):
    base = jax.random.fold_in(key, 23)
    hot_key, source_key = jax.random.split(base)
    hot_row_key, hot_col_key = jax.random.split(hot_key)
    held = CHILDREN * SLOTS
    grid = F // TB
    tile_rows = F // N_ROW // TB
    tile_cols = F // N_COL // TB
    group = N_ROW // N_COL
    half = CAP // 2
    hot_row = jax.random.randint(hot_row_key, (), 0, N_ROW, dtype=jnp.int32)
    hot_shift = jax.random.randint(hot_col_key, (), 0, N_COL - 1, dtype=jnp.int32)
    hot_col = (hot_row // group + 1 + hot_shift) % N_COL
    hottest = hot_row * N_COL + hot_col
    pre_row = hot_col * group + hot_row % group
    pre_col = hot_row // group
    preimage = pre_row * N_COL + pre_col
    skip = (preimage - hottest - 1) % DEVICES

    def one_source(source):
        order_key, row_key, col_key = jax.random.split(source, 3)
        order = jax.random.permutation(order_key, (DEVICES - 2) * half).astype(jnp.int32) // half
        shifted = order + (order >= skip).astype(jnp.int32)
        others = (hottest + 1 + shifted) % DEVICES
        owners = jnp.concatenate([jnp.full((half,), hottest, jnp.int32), jnp.full((half,), preimage, jnp.int32), others[:held - 2 * half]])
        owner_row = owners // N_COL
        owner_col = owners % N_COL
        rows_in = jax.random.randint(row_key, (held,), 0, tile_rows, dtype=jnp.int32)
        cols_in = jax.random.randint(col_key, (held,), 0, tile_rows, dtype=jnp.int32)
        target_row = owner_row * tile_rows + rows_in
        target_col = owner_col * tile_cols + owner_row % group * tile_rows + cols_in
        return target_row * grid + target_col
    return jax.vmap(one_source)(jax.random.split(source_key, DEVICES)).reshape(-1).astype(jnp.int32)


def set_ends(values, key, least, largest):
    spot = [jax.random.randint(jax.random.fold_in(key, axis), (), 0, length) for axis, length in enumerate(values.shape)]
    main_axis = values.shape.index(max(values.shape))
    neighbour = spot[:main_axis] + [(spot[main_axis] + 1) % values.shape[main_axis]] + spot[main_axis + 1:]
    return values.at[tuple(spot)].set(least).at[tuple(neighbour)].set(largest)


def steps_of(stream_key, shape, cuts, smallest, high):
    def one(dim, blocks):
        heights = jax.random.uniform(jax.random.fold_in(jax.random.fold_in(stream_key, 6), dim), (blocks,), jnp.float32, smallest / len(cuts), high / len(cuts))
        return jnp.repeat(jnp.exp(heights), shape[dim] // blocks).reshape((-1,) + (1,) * (len(shape) - dim - 1))

    loudness = one(*cuts[0])
    for cut in cuts[1:]:
        loudness = loudness * one(*cut)
    return loudness


def gaussian(stream_key, dims, width, bound, shards=(), kind=jnp.bfloat16):
    entries = jax.random.normal(stream_key, dims, jnp.float32) * width
    if len(shards) > 0:
        entries = steps_of(stream_key, dims, shards, -0.22, 0.18) * entries
    return jnp.clip(entries, min=-bound, max=bound).astype(kind)


def setup_inputs(seed: int = 0) -> dict:
    splits = jax.random.split(jax.random.key(seed), 6)
    front = draw_front(jax.random.fold_in(splits[5], 71), 0)
    child_tiles = gaussian(splits[1], (DEVICES * CHILDREN * SLOTS, TB * TB), 0.03, 0.4375, ((0, 32),), jnp.float32)
    tile_target = draw_tile_target(jax.random.fold_in(splits[5], 71), 0)
    tile_count = set_ends(jax.random.randint(splits[3], (DEVICES * CHILDREN,), SLOTS - SLOTS // 4, SLOTS + 1), jax.random.fold_in(splits[3], 1), SLOTS - SLOTS // 4, SLOTS).astype(jnp.int32)
    probe = gaussian(splits[4], (F, SK), 0.12, 1.75, ((0, 4),), jnp.float32)
    return dict(front=front, child_tiles=child_tiles, tile_target=tile_target, tile_count=tile_count, probe=probe)


HIGH = lax.Precision.HIGHEST

def reference(front, child_tiles, tile_target, tile_count, probe):
    grid = F // TB
    index = jnp.arange(DEVICES * CHILDREN * SLOTS, dtype=jnp.int32)
    live = index % SLOTS < tile_count[index // SLOTS]
    weighted = jnp.where(live[:, None], child_tiles, jnp.zeros_like(child_tiles))
    squares = weighted.reshape(-1, TB, TB)
    tile_row = tile_target // grid
    tile_col = tile_target % grid
    blocks = jnp.zeros((grid, grid, TB, TB), front.dtype)
    blocks = blocks.at[tile_row, tile_col].add(squares)
    blocks = blocks.at[tile_col, tile_row].add(squares.transpose(0, 2, 1))
    extend = blocks.transpose(0, 2, 1, 3).reshape(F, F)
    matrix = front + extend
    factors = []
    for k in range(PANELS):
        low = k * NB
        high = low + NB
        diag_block = matrix[low:high, low:high]
        chol = jnp.linalg.cholesky(0.5 * (diag_block + diag_block.T))
        below = matrix[low:, low:high]
        solved = jax.scipy.linalg.solve_triangular(chol, below.T, lower=True).T
        factors.append(jnp.pad(solved, ((low, 0), (0, 0))))
        trail = solved[NB:]
        matrix = matrix.at[high:, high:].add(-jnp.dot(trail, trail.T, precision=HIGH))
    panel_factor = jnp.concatenate(factors, axis=1)
    start = PANELS * NB
    lower_part = jnp.dot(matrix[start:, start:], probe[start:], precision=HIGH)
    sketch = jnp.pad(lower_part, ((start, 0), (0, 0)))
    return (panel_factor, sketch)
```

```python
import functools

import jax
import jax.numpy as jnp
from jax import lax
from jax.experimental import pallas as pl
from jax.experimental.pallas import tpu as pltpu
from jax.sharding import PartitionSpec as P

NB = 512
PANELS = 2
PD = NB * PANELS
TB = 64
SLOTS = 32
LANES = 128
NBLK = PD // LANES
PACKED = NBLK * (NBLK + 1) // 2
AXES = ("row", "col")
HIGH = lax.Precision.HIGHEST
MIB = 1 << 20


def block_index(r, c):
    return r * NBLK - r * (r - 1) // 2 + (c - r)


def left_half(shape):
    return lax.broadcasted_iota(jnp.int32, shape, len(shape) - 1) < TB


def add_tile(ref, row, col, half, packed):
    turned = pltpu.roll(packed, TB, 1)
    mask = left_half(packed.shape) == (half == 0)
    top = jnp.where(mask, jnp.where(half == 0, packed, turned), 0.0)
    low = jnp.where(mask, jnp.where(half == 0, turned, packed), 0.0)
    cols = pl.ds(pl.multiple_of(col, LANES), LANES)
    upper = pl.ds(pl.multiple_of(row, TB), TB // 2)
    lower = pl.ds(pl.multiple_of(row + TB // 2, TB // 2), TB // 2)
    ref[upper, cols] += top
    ref[lower, cols] += low


def prepare_kernel(
    held, devices, capacity, local_rows,
    live_ref, row_ref, col_ref, owner_ref, place_ref, me_ref,
    tiles_ref, front_ref,
    out_ref, landing_ref, diag_ref,
    flat_ref, pair_ref, count_ref, slot_ref,
):
    half = TB // 2
    for d in range(devices):
        count_ref[d] = 0

    def clear(s, carry):
        landing_ref[s] = -1
        return carry

    lax.fori_loop(0, devices * capacity, clear, 0)

    def spread(g, carry):
        rows = tiles_ref[pl.ds(pl.multiple_of(g * 8, 8), 8), :]
        for k in range(half):
            flat_ref[pl.ds(g * 8 * half + k, 8, stride=half), :] = rows[:, k * LANES : (k + 1) * LANES]
        return carry

    lax.fori_loop(0, held // 8, spread, 0)

    def assign(t, carry):
        for m in range(2):
            owner = owner_ref[m * held + t]
            slot = owner * capacity + count_ref[owner]
            count_ref[owner] += 1
            slot_ref[m * held + t] = slot
            landing_ref[slot] = jnp.where(live_ref[t] == 1, place_ref[m * held + t], -1)
        return carry

    lax.fori_loop(0, held, assign, 0)

    def quad(q, carry):
        left = left_half((half, LANES))
        naturals = []
        for p in range(2):
            a = flat_ref[pl.ds(pl.multiple_of((4 * q + 2 * p) * half, half), half), :]
            b = flat_ref[pl.ds(pl.multiple_of((4 * q + 2 * p + 1) * half, half), half), :]
            pair_ref[p, pl.ds(0, half, stride=2), :] = jnp.where(left, a, pltpu.roll(b, TB, 1))
            pair_ref[p, pl.ds(1, half, stride=2), :] = jnp.where(left, pltpu.roll(a, TB, 1), b)
            naturals.append(pair_ref[p, :, :])
        turned = jnp.concatenate(naturals, axis=0).T
        for m, values, order in (
            (0, naturals[0], (0, 1)),
            (0, naturals[1], (2, 3)),
            (1, turned[:TB], (0, 2)),
            (1, turned[TB:], (1, 3)),
        ):
            up, low = values[:half], values[half:]
            out_ref[slot_ref[m * held + 4 * q + order[0]]] = jnp.where(left, up, pltpu.roll(low, TB, 1))
            out_ref[slot_ref[m * held + 4 * q + order[1]]] = jnp.where(left, pltpu.roll(up, TB, 1), low)
        return carry

    lax.fori_loop(0, held // 4, quad, 0)

    for r64 in range(PD // TB):
        home = (r64 * TB) // local_rows
        start = r64 * TB - home * local_rows
        mine = (me_ref[0] == home) & (me_ref[1] == 0)
        r = r64 // 2
        for c in range(r, NBLK):
            base = block_index(r, c) * LANES + (r64 % 2) * TB
            piece = front_ref[start : start + TB, c * LANES : (c + 1) * LANES]
            diag_ref[base : base + TB, :] = jnp.where(mine, piece, 0.0)

    def diagonal(t, carry):
        r, c = row_ref[t], col_ref[t]

        @pl.when((live_ref[t] == 1) & (r < PD // TB) & (c < PD // TB))
        def _():
            for m, (a, b) in enumerate(((r, c), (c, r))):
                big, wide = a // 2, b // 2

                @pl.when(wide >= big)
                def _():
                    base = block_index(big, wide) * LANES + (a % 2) * TB
                    add_tile(diag_ref, base, 0, b % 2, out_ref[slot_ref[m * held + t]])

        return carry

    lax.fori_loop(0, held, diagonal, 0)


def prepare(live, first_row, first_col, owner, place, me, child_tiles, front, devices, capacity):
    held = child_tiles.shape[0]
    local_rows, local_cols = front.shape
    half = TB // 2
    smem = pl.BlockSpec(memory_space=pltpu.SMEM)
    rows = min(PD, local_rows)
    return pl.pallas_call(
        functools.partial(prepare_kernel, held, devices, capacity, local_rows),
        grid=(1,),
        out_shape=(
            jax.ShapeDtypeStruct((devices * capacity, half, LANES), jnp.float32),
            jax.ShapeDtypeStruct((devices * capacity,), jnp.int32),
            jax.ShapeDtypeStruct((PACKED * LANES, LANES), jnp.float32),
        ),
        in_specs=[smem] * 6
        + [
            pl.BlockSpec((held, TB * TB), lambda i: (0, 0)),
            pl.BlockSpec((rows, PD), lambda i: (0, 0)),
        ],
        out_specs=(
            pl.BlockSpec((devices * capacity, half, LANES), lambda i: (0, 0, 0)),
            smem,
            pl.BlockSpec((PACKED * LANES, LANES), lambda i: (0, 0)),
        ),
        scratch_shapes=[
            pltpu.VMEM((held * half, LANES), jnp.float32),
            pltpu.VMEM((2, TB, LANES), jnp.float32),
            pltpu.SMEM((devices,), jnp.int32),
            pltpu.SMEM((2 * held,), jnp.int32),
        ],
        compiler_params=pltpu.CompilerParams(vmem_limit_bytes=40 * MIB),
        name="prepare",
    )(live, first_row, first_col, owner, place, me, child_tiles, front)


def lane_splat(x, lane):
    return jnp.broadcast_to(x[:, lane : lane + 1], x.shape)


def row_splat(x, row):
    return jnp.broadcast_to(x[row : row + 1, :], x.shape)


def inverse_factor(strips):
    strips = list(strips)
    lane = lax.broadcasted_iota(jnp.int32, (8, LANES), 1)
    sub = lax.broadcasted_iota(jnp.int32, (8, LANES), 0)
    result = []
    for k in range(LANES // 8):
        strip = strips[k]
        columns = [lane_splat(strip, 8 * k + t) for t in range(8)]
        e = [[row_splat(columns[t], s) if s <= t else None for t in range(8)] for s in range(8)]
        low = [[None] * 8 for _ in range(8)]
        inv = [None] * 8
        for s in range(8):
            x = e[s][s]
            y = lax.rsqrt(x)
            inv[s] = y * (1.5 - 0.5 * x * y * y)
            for t in range(s + 1, 8):
                low[t][s] = e[s][t] * inv[s]
            for t in range(s + 1, 8):
                for u in range(t, 8):
                    e[t][u] = e[t][u] - low[t][s] * low[u][s]
        li = [[None] * 8 for _ in range(8)]
        for s in range(8):
            li[s][s] = inv[s]
            for r in range(s + 1, 8):
                total = low[r][s] * li[s][s]
                for q in range(s + 1, r):
                    total = total + low[r][q] * li[q][s]
                li[r][s] = -inv[r] * total
        inside = (lane >= 8 * k) & (lane < 8 * k + 8)
        unit = jnp.where(lane - 8 * k == sub, 1.0, 0.0)
        strip = jnp.where(inside, unit, strip)
        rows = [row_splat(strip, s) for s in range(8)]
        u = []
        for r in range(8):
            total = li[r][0] * rows[0]
            for s in range(1, r + 1):
                total = total + li[r][s] * rows[s]
            u.append(total)
        mine = u[0]
        for r in range(1, 8):
            mine = jnp.where(sub == r, u[r], mine)
        result.append(jnp.where(lane < 8 * k + 8, mine, 0.0))
        if k + 1 == LANES // 8:
            break
        v = []
        for s in range(8):
            total = li[s][s] * u[s]
            for r in range(s + 1, 8):
                total = total + li[r][s] * u[r]
            v.append(total)
        for i in range(k + 1, LANES // 8):
            old = strips[i]
            total = lane_splat(old, 8 * k) * v[0]
            for s in range(1, 8):
                total = total + lane_splat(old, 8 * k + s) * v[s]
            strips[i] = jnp.where(inside, 0.0, old) - total
    return result


def factor_kernel(packed_ref, out_ref, top_ref, small_ref):
    out_ref[...] = jnp.zeros_like(out_ref)
    for r in range(NBLK):
        for c in range(r, NBLK):
            base = block_index(r, c) * LANES
            out_ref[r * LANES : (r + 1) * LANES, c * LANES : (c + 1) * LANES] = packed_ref[base : base + LANES, :]

    eye = jnp.where(
        lax.broadcasted_iota(jnp.int32, (LANES, LANES), 0) == lax.broadcasted_iota(jnp.int32, (LANES, LANES), 1), 1.0, 0.0
    )

    def outer(k, carry):
        at = pl.multiple_of(k * LANES, LANES)
        here = pl.ds(at, LANES)
        block = out_ref[here, here]
        block = 0.5 * (block + block.T)
        small_ref[...] = block
        strips = inverse_factor([small_ref[8 * i : 8 * i + 8, :] for i in range(LANES // 8)])
        for i, strip in enumerate(strips):
            small_ref[8 * i : 8 * i + 8, :] = strip
        out_ref[here, here] = eye
        top = jnp.dot(small_ref[...], out_ref[here, :], precision=HIGH, preferred_element_type=jnp.float32)
        top_ref[...] = top
        column = lax.broadcasted_iota(jnp.int32, (LANES, PD), 1)
        out_ref[here, :] = jnp.where(column < at + LANES, top, 0.0)

        def trailing(i, carry):
            there = pl.ds(pl.multiple_of(i * LANES, LANES), LANES)
            out_ref[there, here] = jnp.zeros((LANES, LANES), jnp.float32)
            out_ref[there, :] -= lax.dot_general(
                top_ref[:, there], top_ref[...], (((0,), (0,)), ((), ())), precision=HIGH, preferred_element_type=jnp.float32
            )
            return carry

        lax.fori_loop(k + 1, NBLK, trailing, 0)
        return carry

    lax.fori_loop(0, NBLK, outer, 0)


def inverse_of_factor(packed):
    return pl.pallas_call(
        factor_kernel,
        out_shape=jax.ShapeDtypeStruct((PD, PD), jnp.float32),
        in_specs=[pl.BlockSpec(memory_space=pltpu.VMEM)],
        out_specs=pl.BlockSpec(memory_space=pltpu.VMEM),
        scratch_shapes=[pltpu.VMEM((LANES, PD), jnp.float32), pltpu.VMEM((LANES, LANES), jnp.float32)],
        compiler_params=pltpu.CompilerParams(vmem_limit_bytes=24 * MIB),
        name="factor",
    )(packed)


def split(x):
    high = x.astype(jnp.bfloat16)
    return high, (x - high.astype(jnp.float32)).astype(jnp.bfloat16)


def assemble_kernel(
    slots, row_chunk, width,
    tile_row_ref, tile_col_ref, first_ref,
    front_ref, incoming_ref, probe_ref,
    product_ref, panel_ref,
    matrix_ref, high_ref, low_ref, semaphore,
):
    copy = pltpu.make_async_copy(front_ref, matrix_ref, semaphore)
    copy.start()
    depth = probe_ref.shape[0]
    step = 256
    first = first_ref[0]

    def cut(s, carry):
        rows = pl.ds(pl.multiple_of(s * step, step), step)
        index = lax.broadcasted_iota(jnp.int32, (step, probe_ref.shape[1]), 0) + s * step
        high, low = split(jnp.where(index >= first, probe_ref[rows, :], 0.0))
        high_ref[rows, :] = high
        low_ref[rows, :] = low
        return carry

    lax.fori_loop(0, depth // step, cut, 0)
    copy.wait()

    def place(s, carry):
        r, c = tile_row_ref[s], tile_col_ref[s]

        @pl.when(r >= 0)
        def _():
            add_tile(matrix_ref, r * TB, (c // 2) * LANES, c % 2, incoming_ref[s])

        return carry

    lax.fori_loop(0, slots, place, 0)

    def multiply(b, carry):
        rows = pl.ds(pl.multiple_of(b * row_chunk, row_chunk), row_chunk)
        panel_ref[rows, :] = matrix_ref[rows, :PD]
        high, low = split(matrix_ref[rows, :])
        dot = functools.partial(jnp.dot, preferred_element_type=jnp.float32)
        total = dot(high, high_ref[...]) + (dot(high, low_ref[...]) + dot(low, high_ref[...]))
        for j in range(probe_ref.shape[1] // width):
            product_ref[j, rows, :] = total[:, j * width : (j + 1) * width]
        return carry

    lax.fori_loop(0, matrix_ref.shape[0] // row_chunk, multiply, 0)


def assemble(tile_row, tile_col, first, front, incoming, probe, col_count):
    local_rows, local_cols = front.shape
    columns = probe.shape[1]
    width = columns // col_count
    smem = pl.BlockSpec(memory_space=pltpu.SMEM)
    vmem = pl.BlockSpec(memory_space=pltpu.VMEM)
    row_chunk = 192 if local_rows % 192 == 0 else 64
    return pl.pallas_call(
        functools.partial(assemble_kernel, tile_row.shape[0], row_chunk, width),
        out_shape=(
            jax.ShapeDtypeStruct((col_count, local_rows, width), jnp.float32),
            jax.ShapeDtypeStruct((local_rows, PD), jnp.float32),
        ),
        in_specs=[smem] * 3 + [pl.BlockSpec(memory_space=pl.ANY), vmem, vmem],
        out_specs=(vmem, vmem),
        scratch_shapes=[
            pltpu.VMEM((local_rows, local_cols), jnp.float32),
            pltpu.VMEM((local_cols, columns), jnp.bfloat16),
            pltpu.VMEM((local_cols, columns), jnp.bfloat16),
            pltpu.SemaphoreType.DMA,
        ],
        compiler_params=pltpu.CompilerParams(vmem_limit_bytes=56 * MIB),
        name="assemble",
    )(tile_row, tile_col, first, front, incoming, probe)


def masks(count):
    return [1 << b for b in range(count.bit_length() - 1)]


def exchange(x, axis, mask, count):
    return lax.ppermute(x, axis, [(d, d ^ mask) for d in range(count)])


def choose(bit, x):
    h = x.shape[0] // 2
    return jnp.where(bit, x[h:], x[:h]), jnp.where(bit, x[:h], x[h:])


def halve(x, axis, index, mask, count):
    keep, send = choose((index & mask) != 0, x)
    return keep + exchange(send, axis, mask, count)


def double(x, axis, index, mask, count):
    other = exchange(x, axis, mask, count)
    bit = (index & mask) != 0
    return jnp.concatenate([jnp.where(bit, other, x), jnp.where(bit, x, other)], axis=0)


def all_sum(x, axis, index, order, count):
    for mask in order:
        x = halve(x, axis, index, mask, count)
    for mask in order[::-1]:
        x = double(x, axis, index, mask, count)
    return x


def spread(x, axis, index, order, count):
    for mask in order:
        other = lax.ppermute(x, axis, [(d, d + mask) for d in range(0, count, 2 * mask)])
        x = jnp.where((index & (2 * mask - 1)) == mask, other, x)
    return x


def per_device(front, child_tiles, tile_target, tile_count, probe):
    row_count = lax.axis_size("row")
    col_count = lax.axis_size("col")
    devices = row_count * col_count
    local_rows, local_cols = front.shape
    tile_rows = local_rows // TB
    tile_cols = local_cols // TB
    grid = tile_cols * col_count
    held = child_tiles.shape[0]
    capacity = 2 * max(1, (held + devices - 1) // devices)
    row_index = lax.axis_index("row")
    col_index = lax.axis_index("col")
    device = row_index * col_count + col_index

    slot_index = jnp.arange(held, dtype=jnp.int32)
    live = (slot_index % SLOTS < tile_count[slot_index // SLOTS]).astype(jnp.int32)
    first_row = tile_target // grid
    first_col = tile_target % grid
    target_row = jnp.concatenate([first_row, first_col])
    target_col = jnp.concatenate([first_col, first_row])
    owner = target_row // tile_rows * col_count + target_col // tile_cols
    place = target_row % tile_rows * tile_cols + target_col % tile_cols
    me = jnp.stack([row_index, col_index])
    outgoing, landing, diagonal = prepare(
        live, first_row, first_col, owner, place, me, child_tiles, front, devices, capacity
    )

    packed = all_sum(diagonal, AXES, device, masks(devices), devices)

    places = lax.all_to_all(landing.reshape(devices, capacity), AXES, split_axis=0, concat_axis=0, tiled=True).reshape(-1)
    incoming = lax.all_to_all(
        outgoing.reshape(devices, capacity, TB // 2, LANES), AXES, split_axis=0, concat_axis=0, tiled=True
    ).reshape(devices * capacity, TB // 2, LANES)

    inverse = inverse_of_factor(packed)

    col_start = col_index * local_cols
    first = jnp.clip(PD - col_start, 0, local_cols).reshape(1)
    tile_row = jnp.where(places >= 0, places // tile_cols, -1)
    product, panel = assemble(tile_row, places % tile_cols, first, front, incoming, probe, col_count)

    share = product.reshape(-1, product.shape[2])
    order = masks(col_count)[::-1]
    for mask in order:
        share = halve(share, "col", col_index, mask, col_count)

    panel = spread(panel, "col", col_index, masks(col_count)[::-1], col_count)

    pieces = []
    for home in range((PD + local_rows - 1) // local_rows):
        rows = min(PD - home * local_rows, local_rows)
        pieces.append(jnp.where(row_index == home, share[:rows], 0.0))
    if len(pieces) == 1:
        top = spread(pieces[0], "row", row_index, masks(row_count)[::-1], row_count)
    else:
        top = all_sum(jnp.concatenate(pieces, axis=0), "row", row_index, masks(row_count), row_count)

    dot = functools.partial(jnp.dot, precision=lax.Precision.HIGH, preferred_element_type=jnp.float32)
    width = PD // col_count
    mine = lax.dynamic_slice_in_dim(inverse, col_index * width, width, 0)
    solved = lax.dot_general(
        panel, mine, (((1,), (1,)), ((), ())), precision=lax.Precision.HIGH, preferred_element_type=jnp.float32
    )
    global_rows = row_index * local_rows + jnp.arange(local_rows, dtype=jnp.int32)
    panel_of = (col_index * width + jnp.arange(width, dtype=jnp.int32)) // NB
    panel_factor = jnp.where(global_rows[:, None] >= panel_of[None, :] * NB, solved, 0.0)

    weights = lax.dot_general(
        inverse, dot(inverse, top), (((0,), (0,)), ((), ())), precision=lax.Precision.HIGH, preferred_element_type=jnp.float32
    )
    sketch = jnp.where((global_rows >= PD)[:, None], share - dot(panel, weights), 0.0)
    return (panel_factor, sketch)


def solution(mesh):
    return jax.shard_map(
        per_device,
        mesh=mesh,
        in_specs=(
            P("row", "col"),
            P(("row", "col"), None),
            P(("row", "col")),
            P(("row", "col")),
            P("col", None),
        ),
        out_specs=(P("row", "col"), P("row", "col")),
        check_vma=False,
    )
```

```python
import functools

import jax
import jax.numpy as jnp
import numpy as np
from jax import lax
from jax.experimental import pallas as pl
from jax.experimental.pallas import tpu as pltpu
from jax.sharding import PartitionSpec as P

NB = 512
PANELS = 2
PD = NB * PANELS
TB = 64
SLOTS = 32
LANES = 128
NBLK = PD // LANES
PACKED = NBLK * (NBLK + 1) // 2
AXES = ("row", "col")
HIGH = lax.Precision.HIGHEST
MIB = 1 << 20
PIECES = 3


def block_index(r, c):
    return r * (r + 1) // 2 + c


def left_half(shape):
    return lax.broadcasted_iota(jnp.int32, shape, len(shape) - 1) < TB


def magic(divisor, limit):
    x = np.arange(limit, dtype=np.int64)
    for shift in range(8, 31):
        m = (1 << shift) // divisor + 1
        if m * limit < 1 << 31 and np.array_equal((x * m) >> shift, x // divisor):
            return m, shift
    raise ValueError("no multiplier")


def quotient(x, divisor, limit):
    m, shift = magic(divisor, limit)
    return (x * m) >> shift


def is_live(count_ref, t):
    return t % SLOTS < count_ref[t // SLOTS]


def pick_kernel(
    held, most, grid,
    target_ref, count_ref,
    tiles_ref,
    out_ref,
    flat_ref, pair_ref, label_ref, filled_ref,
):
    half = TB // 2
    side = PD // TB
    filled_ref[0] = 0
    for s in range(most):
        label_ref[s] = -1

    def look(t, carry):
        r = quotient(target_ref[t], grid, grid * grid)
        c = target_ref[t] - r * grid

        @pl.when(is_live(count_ref, t) & (r < side) & (c < side))
        def _():
            left = left_half((half, LANES))
            group = tiles_ref[pl.ds(pl.multiple_of(t // 8 * 8, 8), 8), :]
            row = lax.broadcasted_iota(jnp.int32, group.shape, 0)
            line = jnp.sum(jnp.where(row == t % 8, group, 0.0), axis=0, keepdims=True)
            for k in range(half):
                flat_ref[k : k + 1, :] = line[:, k * LANES : (k + 1) * LANES]
            flat = flat_ref[...]
            turned = pltpu.roll(flat, TB, 1)
            pair_ref[pl.ds(0, half, stride=2), :] = jnp.where(left, flat, turned)
            pair_ref[pl.ds(1, half, stride=2), :] = jnp.where(left, turned, flat)
            natural = pair_ref[...]
            mirrored = natural.T[:TB]
            mirrored = jnp.concatenate([mirrored, mirrored], axis=1)
            swap = r // 2 > c // 2
            value = jnp.where(swap, mirrored, natural) * jnp.where(r // 2 == c // 2, 2.0, 1.0)
            filled = filled_ref[0]
            out_ref[pl.ds(pl.multiple_of(filled * half, half), half), :] = jnp.where(left, value[:half], pltpu.roll(value[half:], TB, 1))
            label_ref[filled] = jnp.where(swap, c * side + r, r * side + c)
            filled_ref[0] = filled + 1

        return carry

    lax.fori_loop(0, held, look, 0)
    lane = lax.broadcasted_iota(jnp.int32, (8, LANES), 1)
    line = jnp.full((8, LANES), -1, jnp.int32)
    for s in range(most):
        line = jnp.where(lane == s, label_ref[s], line)
    out_ref[most * half : most * half + 8, :] = line.astype(jnp.float32)


def pick(target, count, child_tiles, most, grid):
    held = child_tiles.shape[0]
    smem = pl.BlockSpec(memory_space=pltpu.SMEM)
    rows = most * TB // 2 + 8
    return pl.pallas_call(
        functools.partial(pick_kernel, held, most, grid),
        grid=(1,),
        out_shape=jax.ShapeDtypeStruct((rows, LANES), jnp.float32),
        in_specs=[smem] * 2 + [pl.BlockSpec((held, TB * TB), lambda i: (0, 0))],
        out_specs=pl.BlockSpec((rows, LANES), lambda i: (0, 0)),
        scratch_shapes=[
            pltpu.VMEM((TB // 2, LANES), jnp.float32),
            pltpu.VMEM((TB, LANES), jnp.float32),
            pltpu.SMEM((most,), jnp.int32),
            pltpu.SMEM((1,), jnp.int32),
        ],
        compiler_params=pltpu.CompilerParams(vmem_limit_bytes=16 * MIB),
        name="pick",
    )(target, count, child_tiles)


def stage_kernel(
    held, devices, capacity, grid, tile_rows, tile_cols, col_count,
    target_ref, tally_ref,
    tiles_ref,
    out_ref,
    flat_ref, pair_ref, count_ref, slot_ref, landing_ref,
):
    half = TB // 2
    for d in range(devices):
        count_ref[d] = 0

    def clear(s, carry):
        landing_ref[s] = -1
        return carry

    lax.fori_loop(0, devices * capacity, clear, 0)

    def spread_out(g, carry):
        rows = tiles_ref[pl.ds(pl.multiple_of(g * 8, 8), 8), :]
        for k in range(half):
            flat_ref[pl.ds(g * 8 * half + k, 8, stride=half), :] = rows[:, k * LANES : (k + 1) * LANES]
        return carry

    lax.fori_loop(0, held // 8, spread_out, 0)

    def assign(t, carry):
        alive = is_live(tally_ref, t)
        r = quotient(target_ref[t], grid, grid * grid)
        c = target_ref[t] - r * grid
        for m, (a, b) in enumerate(((r, c), (c, r))):
            home = quotient(a, tile_rows, grid)
            side = quotient(b, tile_cols, grid)
            owner = home * col_count + side
            place = (a - home * tile_rows) * tile_cols + (b - side * tile_cols)
            filled = count_ref[owner]
            count_ref[owner] = filled + 1
            slot = owner * capacity + filled
            slot_ref[m * held + t] = owner * (capacity * half + 8) + filled * half
            landing_ref[slot] = jnp.where(alive, place, -1)
        return carry

    lax.fori_loop(0, held, assign, 0, unroll=4)

    def put(index, value):
        out_ref[pl.ds(pl.multiple_of(slot_ref[index], 8), half), :] = value

    def quad(q, carry):
        left = left_half((half, LANES))
        naturals = []
        for p in range(2):
            a = flat_ref[pl.ds(pl.multiple_of((4 * q + 2 * p) * half, half), half), :]
            b = flat_ref[pl.ds(pl.multiple_of((4 * q + 2 * p + 1) * half, half), half), :]
            pair_ref[p, pl.ds(0, half, stride=2), :] = jnp.where(left, a, pltpu.roll(b, TB, 1))
            pair_ref[p, pl.ds(1, half, stride=2), :] = jnp.where(left, pltpu.roll(a, TB, 1), b)
            naturals.append(pair_ref[p, :, :])
        turned = jnp.concatenate(naturals, axis=0).T
        for m, values, order in (
            (0, naturals[0], (0, 1)),
            (0, naturals[1], (2, 3)),
            (1, turned[:TB], (0, 2)),
            (1, turned[TB:], (1, 3)),
        ):
            up, low = values[:half], values[half:]
            put(m * held + 4 * q + order[0], jnp.where(left, up, pltpu.roll(low, TB, 1)))
            put(m * held + 4 * q + order[1], jnp.where(left, pltpu.roll(up, TB, 1), low))
        return carry

    lax.fori_loop(0, held // 4, quad, 0, unroll=2)

    lane = lax.broadcasted_iota(jnp.int32, (8, LANES), 1)

    def label(d, carry):
        line = jnp.full((8, LANES), -1, jnp.int32)
        for s in range(capacity):
            line = jnp.where(lane == s, landing_ref[d * capacity + s], line)
        at = d * (capacity * half + 8) + capacity * half
        out_ref[pl.ds(pl.multiple_of(at, 8), 8), :] = line.astype(jnp.float32)
        return carry

    lax.fori_loop(0, devices, label, 0)


def stage(target, tally, child_tiles, devices, capacity, grid, tile_rows, tile_cols, col_count):
    held = child_tiles.shape[0]
    half = TB // 2
    smem = pl.BlockSpec(memory_space=pltpu.SMEM)
    rows = devices * (capacity * half + 8)
    return pl.pallas_call(
        functools.partial(stage_kernel, held, devices, capacity, grid, tile_rows, tile_cols, col_count),
        grid=(1,),
        out_shape=jax.ShapeDtypeStruct((rows, LANES), jnp.float32),
        in_specs=[smem] * 2 + [pl.BlockSpec((held, TB * TB), lambda i: (0, 0))],
        out_specs=pl.BlockSpec((rows, LANES), lambda i: (0, 0)),
        scratch_shapes=[
            pltpu.VMEM((held * half, LANES), jnp.float32),
            pltpu.VMEM((2, TB, LANES), jnp.float32),
            pltpu.SMEM((devices,), jnp.int32),
            pltpu.SMEM((2 * held,), jnp.int32),
            pltpu.SMEM((devices * capacity,), jnp.int32),
        ],
        compiler_params=pltpu.CompilerParams(vmem_limit_bytes=24 * MIB),
        name="stage",
    )(target, tally, child_tiles)


def split(x):
    high = x.astype(jnp.bfloat16)
    return high, (x - high.astype(jnp.float32)).astype(jnp.bfloat16)


def dot3(left_high, left_low, right_high, right_low):
    dot = functools.partial(jnp.dot, preferred_element_type=jnp.float32)
    return dot(left_high, right_high) + (dot(left_high, right_low) + dot(left_low, right_high))


def lane_splat(x, lane):
    return jnp.broadcast_to(x[:, lane : lane + 1], x.shape)


def row_splat(ref, row):
    return jnp.broadcast_to(ref[row : row + 1, :], (8, LANES))


def inverse_factor(strips, splat_ref):
    strips = list(strips)
    lane = lax.broadcasted_iota(jnp.int32, (8, LANES), 1)
    sub = lax.broadcasted_iota(jnp.int32, (8, LANES), 0)
    result = []
    for k in range(LANES // 8):
        strip = strips[k]
        columns = [lane_splat(strip, 8 * k + t) for t in range(8)]
        for t in range(8):
            splat_ref[8 * t : 8 * t + 8, :] = columns[t]
        e = [[row_splat(splat_ref, 8 * t + s) if s <= t else None for t in range(8)] for s in range(8)]
        low = [[None] * 8 for _ in range(8)]
        inv = [None] * 8
        for s in range(8):
            inv[s] = lax.rsqrt(e[s][s])
            for t in range(s + 1, 8):
                low[t][s] = e[s][t] * inv[s]
            for t in range(s + 1, 8):
                for u in range(t, 8):
                    e[t][u] = e[t][u] - low[t][s] * low[u][s]
        li = [[None] * 8 for _ in range(8)]
        for s in range(8):
            li[s][s] = inv[s]
            for r in range(s + 1, 8):
                total = low[r][s] * li[s][s]
                for q in range(s + 1, r):
                    total = total + low[r][q] * li[q][s]
                li[r][s] = -inv[r] * total
        inside = (lane >= 8 * k) & (lane < 8 * k + 8)
        unit = jnp.where(lane - 8 * k == sub, 1.0, 0.0)
        strip = jnp.where(inside, unit, strip)
        splat_ref[64:72, :] = strip
        rows = [row_splat(splat_ref, 64 + s) for s in range(8)]
        u = []
        for r in range(8):
            total = li[r][0] * rows[0]
            for s in range(1, r + 1):
                total = total + li[r][s] * rows[s]
            u.append(total)
        mine = u[0]
        for r in range(1, 8):
            mine = jnp.where(sub == r, u[r], mine)
        result.append(jnp.where(lane < 8 * k + 8, mine, 0.0))
        if k + 1 == LANES // 8:
            break
        v = []
        for s in range(8):
            total = li[s][s] * u[s]
            for r in range(s + 1, 8):
                total = total + li[r][s] * u[r]
            v.append(total)
        for i in range(k + 1, LANES // 8):
            old = strips[i]
            total = lane_splat(old, 8 * k) * v[0]
            for s in range(1, 8):
                total = total + lane_splat(old, 8 * k + s) * v[s]
            strips[i] = jnp.where(inside, 0.0, old) - total
    return result


def factor_kernel(
    most, senders,
    label_ref, me_ref,
    front_ref, tiles_ref,
    packed_ref,
    out_ref, top_ref, small_ref, high_ref, low_ref, splat_ref, semaphore,
):
    @pl.when(me_ref[0] == 0)
    def _():
        copy = pltpu.make_async_copy(front_ref.at[:PD, :PD], out_ref, semaphore)
        copy.start()
        copy.wait()
        factor(most, senders, label_ref, front_ref, tiles_ref, packed_ref, out_ref, top_ref, small_ref, high_ref, low_ref, splat_ref)


def factor(most, senders, label_ref, front_ref, tiles_ref, packed_ref, out_ref, top_ref, small_ref, high_ref, low_ref, splat_ref):
    half = TB // 2
    side = PD // TB
    for r in range(NBLK):
        rows = slice(r * LANES, (r + 1) * LANES)
        if r > 0:
            out_ref[rows, : r * LANES] = jnp.zeros((LANES, r * LANES), jnp.float32)
    left = left_half((half, LANES))
    group = 8 if most * senders % 8 == 0 else 2

    def place(g, carry):
        parts = []
        for e in range(group):
            s = g * group + e
            p = label_ref[s]
            alive = p >= 0
            p = jnp.clip(p, 0, side * side - 1)
            r, c = p // side, p % side
            even = c % 2 == 0
            source = s // most * (most * half + 8) + s % most * half
            packed = tiles_ref[pl.ds(pl.multiple_of(source, 8), half), :]
            turned = pltpu.roll(packed, TB, 1)
            mask = (left == even) & alive
            top = jnp.where(mask, jnp.where(even, packed, turned), 0.0)
            low = jnp.where(mask, jnp.where(even, turned, packed), 0.0)
            parts.append((r, c // 2, top, low))
        for r, c, top, low in parts:
            cols = pl.ds(pl.multiple_of(c * LANES, LANES), LANES)
            out_ref[pl.ds(pl.multiple_of(r * TB, TB), half), cols] += top
            out_ref[pl.ds(pl.multiple_of(r * TB + half, half), half), cols] += low
        return carry

    lax.fori_loop(0, most * senders // group, place, 0)

    eye = jnp.where(
        lax.broadcasted_iota(jnp.int32, (LANES, LANES), 0) == lax.broadcasted_iota(jnp.int32, (LANES, LANES), 1), 1.0, 0.0
    )

    def outer(k, carry):
        at = pl.multiple_of(k * LANES, LANES)
        here = pl.ds(at, LANES)
        block = out_ref[here, here]
        block = 0.5 * (block + block.T)
        small_ref[...] = block
        strips = inverse_factor([small_ref[8 * i : 8 * i + 8, :] for i in range(LANES // 8)], splat_ref)
        for i, strip in enumerate(strips):
            small_ref[8 * i : 8 * i + 8, :] = strip
        out_ref[here, here] = eye
        top = dot3(*split(small_ref[...]), *split(out_ref[here, :]))
        top_ref[...] = top
        column = lax.broadcasted_iota(jnp.int32, (LANES, PD), 1)
        out_ref[here, :] = jnp.where(column < at + LANES, top, 0.0)
        high_ref[...], low_ref[...] = split(top)
        for step in range(NBLK - 1):

            @pl.when(k == step)
            def _():
                edge = (step + 1) * LANES
                for start in range(edge, PD, LANES):
                    there = slice(start, start + LANES)
                    across = split(top_ref[:, there].T)
                    out_ref[there, :edge] = jnp.where(
                        lax.broadcasted_iota(jnp.int32, (LANES, edge), 1) < edge - LANES, out_ref[there, :edge], 0.0
                    ) - dot3(*across, high_ref[:, :edge], low_ref[:, :edge])
                    out_ref[there, start:] -= dot3(*across, high_ref[:, start:], low_ref[:, start:])

        return carry

    lax.fori_loop(0, NBLK, outer, 0)
    for r in range(NBLK):
        for c in range(r + 1):
            base = block_index(r, c) * LANES
            packed_ref[base : base + LANES, :] = out_ref[r * LANES : (r + 1) * LANES, c * LANES : (c + 1) * LANES]


def inverse_of_factor(label, me, front, tiles, most, senders):
    smem = pl.BlockSpec(memory_space=pltpu.SMEM)
    return pl.pallas_call(
        functools.partial(factor_kernel, most, senders),
        grid=(1,),
        out_shape=jax.ShapeDtypeStruct((PACKED * LANES, LANES), jnp.float32),
        in_specs=[smem, smem, pl.BlockSpec(memory_space=pl.ANY), pl.BlockSpec(tiles.shape, lambda i: (0, 0))],
        out_specs=pl.BlockSpec((PACKED * LANES, LANES), lambda i: (0, 0)),
        scratch_shapes=[
            pltpu.VMEM((PD, PD), jnp.float32),
            pltpu.VMEM((LANES, PD), jnp.float32),
            pltpu.VMEM((LANES, LANES), jnp.float32),
            pltpu.VMEM((LANES, PD), jnp.bfloat16),
            pltpu.VMEM((LANES, PD), jnp.bfloat16),
            pltpu.VMEM((72, LANES), jnp.float32),
            pltpu.SemaphoreType.DMA,
        ],
        compiler_params=pltpu.CompilerParams(vmem_limit_bytes=56 * MIB),
        name="factor",
    )(label, me, front, tiles)


def unpack_kernel(packed_ref, out_ref):
    for r in range(NBLK):
        for c in range(NBLK):
            rows, cols = slice(r * LANES, (r + 1) * LANES), slice(c * LANES, (c + 1) * LANES)
            if c > r:
                out_ref[rows, cols] = jnp.zeros((LANES, LANES), jnp.float32)
            else:
                base = block_index(r, c) * LANES
                out_ref[rows, cols] = packed_ref[base : base + LANES, :]


def unpack(packed):
    vmem = pl.BlockSpec(memory_space=pltpu.VMEM)
    return pl.pallas_call(
        unpack_kernel,
        out_shape=jax.ShapeDtypeStruct((PD, PD), jnp.float32),
        in_specs=[vmem],
        out_specs=vmem,
        compiler_params=pltpu.CompilerParams(vmem_limit_bytes=16 * MIB),
        name="unpack",
    )(packed)


def assemble_kernel(
    slots, capacity, tile_cols, limit, row_chunk, width, order,
    landing_ref, first_ref,
    front_ref, incoming_ref, probe_ref,
    product_ref, *rest,
):
    panels, (matrix_ref, high_ref, low_ref, semaphore) = rest[:-4], rest[-4:]
    copy = pltpu.make_async_copy(front_ref, matrix_ref, semaphore)
    copy.start()
    step = 256 if probe_ref.shape[0] % 256 == 0 else 128
    half = TB // 2

    def cut(s, carry):
        rows = pl.ds(pl.multiple_of(s * step, step), step)
        index = lax.broadcasted_iota(jnp.int32, (step, probe_ref.shape[1]), 0) + s * step
        high, low = split(jnp.where(index >= first_ref[0], probe_ref[rows, :], 0.0))
        high_ref[rows, :] = high
        low_ref[rows, :] = low
        return carry

    lax.fori_loop(0, probe_ref.shape[0] // step, cut, 0)
    copy.wait()
    block = capacity * half + 8
    group = 8 if slots % 8 == 0 else 2
    left = left_half((half, LANES))

    def place(g, carry):
        parts = []
        for e in range(group):
            s = g * group + e
            p = landing_ref[s]
            alive = p >= 0
            p = jnp.maximum(p, 0)
            r = quotient(p, tile_cols, limit)
            c = p - r * tile_cols
            even = c % 2 == 0
            source = s // capacity * block + s % capacity * half
            packed = incoming_ref[pl.ds(pl.multiple_of(source, 8), half), :]
            turned = pltpu.roll(packed, TB, 1)
            mask = (left == even) & alive
            top = jnp.where(mask, jnp.where(even, packed, turned), 0.0)
            low = jnp.where(mask, jnp.where(even, turned, packed), 0.0)
            parts.append((r, c // 2, top, low))
        for r, c, top, low in parts:
            cols = pl.ds(pl.multiple_of(c * LANES, LANES), LANES)
            matrix_ref[pl.ds(pl.multiple_of(r * TB, TB), half), cols] += top
            matrix_ref[pl.ds(pl.multiple_of(r * TB + half, half), half), cols] += low
        return carry

    lax.fori_loop(0, slots // group, place, 0)
    rows = matrix_ref.shape[0] // len(panels)
    for i, panel_ref in enumerate(panels):
        panel_ref[...] = matrix_ref[i * rows : (i + 1) * rows, :PD]

    def multiply(b, carry):
        rows = pl.ds(pl.multiple_of(b * row_chunk, row_chunk), row_chunk)
        high, low = split(matrix_ref[rows, :])
        dot = functools.partial(jnp.dot, preferred_element_type=jnp.float32)
        total = dot(high, high_ref[...]) + (dot(high, low_ref[...]) + dot(low, high_ref[...]))
        for j, at in enumerate(order):
            product_ref[at, rows, :] = total[:, j * width : (j + 1) * width]
        return carry

    lax.fori_loop(0, matrix_ref.shape[0] // row_chunk, multiply, 0)


def assemble(landing, first, front, incoming, probe, capacity, tile_rows, tile_cols, order):
    local_rows, local_cols = front.shape
    columns = probe.shape[1]
    width = columns // len(order)
    smem = pl.BlockSpec(memory_space=pltpu.SMEM)
    vmem = pl.BlockSpec(memory_space=pltpu.VMEM)
    row_chunk = 192 if local_rows % 192 == 0 else 64
    return pl.pallas_call(
        functools.partial(
            assemble_kernel, landing.shape[0], capacity, tile_cols, tile_rows * tile_cols, row_chunk, width, order
        ),
        out_shape=(jax.ShapeDtypeStruct((len(order), local_rows, width), jnp.float32),)
        + (jax.ShapeDtypeStruct((local_rows // PIECES, PD), jnp.float32),) * PIECES,
        in_specs=[smem] * 2 + [pl.BlockSpec(memory_space=pl.ANY), vmem, vmem],
        out_specs=(vmem,) * (1 + PIECES),
        scratch_shapes=[
            pltpu.VMEM((local_rows, local_cols), jnp.float32),
            pltpu.VMEM((local_cols, columns), jnp.bfloat16),
            pltpu.VMEM((local_cols, columns), jnp.bfloat16),
            pltpu.SemaphoreType.DMA,
        ],
        compiler_params=pltpu.CompilerParams(vmem_limit_bytes=56 * MIB),
        name="assemble",
    )(landing, first, front, incoming, probe)


def finish_kernel(
    sources, width,
    where_ref, *refs,
):
    panels = refs[: sources * PIECES]
    inverse_ref, weights_ref, share_ref, solved_ref, sketch_ref, panel_ref, semaphore = refs[sources * PIECES :]
    col, row_start = where_ref[0], where_ref[1]
    piece = panel_ref.shape[0] // PIECES
    for j in range(sources):

        @pl.when(col == j)
        def _():
            moves = [
                pltpu.make_async_copy(panels[j * PIECES + i], panel_ref.at[i * piece : (i + 1) * piece], semaphore.at[i])
                for i in range(PIECES)
            ]
            for move in moves:
                move.start()
            for move in moves:
                move.wait()

    right_high, right_low = split(jnp.concatenate([inverse_ref[...].T, weights_ref[...]], axis=1))
    dot = functools.partial(jnp.dot, preferred_element_type=jnp.float32)
    step = 192 if panel_ref.shape[0] % 192 == 0 else 64

    def body(b, carry):
        rows = pl.ds(pl.multiple_of(b * step, step), step)
        high, low = split(panel_ref[rows, :])
        total = dot(high, right_high) + (dot(high, right_low) + dot(low, right_high))
        index = row_start + b * step + lax.broadcasted_iota(jnp.int32, (step, width), 0)
        column = col * width + lax.broadcasted_iota(jnp.int32, (step, width), 1)
        solved_ref[rows, :] = jnp.where(index >= (column // NB) * NB, total[:, :width], 0.0)
        rest = share_ref[rows, :] - total[:, width:]
        index = row_start + b * step + lax.broadcasted_iota(jnp.int32, rest.shape, 0)
        sketch_ref[rows, :] = jnp.where(index >= PD, rest, 0.0)
        return carry

    lax.fori_loop(0, panel_ref.shape[0] // step, body, 0)


def finish(where, panels, inverse, weights, share):
    local_rows = share.shape[0]
    width = inverse.shape[0]
    vmem = pl.BlockSpec(memory_space=pltpu.VMEM)
    return pl.pallas_call(
        functools.partial(finish_kernel, len(panels), width),
        out_shape=(
            jax.ShapeDtypeStruct((local_rows, width), jnp.float32),
            jax.ShapeDtypeStruct(share.shape, jnp.float32),
        ),
        in_specs=[pl.BlockSpec(memory_space=pltpu.SMEM)] + [pl.BlockSpec(memory_space=pl.ANY)] * (len(panels) * PIECES) + [vmem] * 3,
        out_specs=(vmem, vmem),
        scratch_shapes=[pltpu.VMEM((local_rows, PD), jnp.float32), pltpu.SemaphoreType.DMA((PIECES,))],
        compiler_params=pltpu.CompilerParams(vmem_limit_bytes=28 * MIB),
        name="finish",
    )(where, *sum(panels, []), inverse, weights, share)


def masks(count):
    return [1 << b for b in range(count.bit_length() - 1)]


def exchange(x, axis, mask, count):
    return lax.ppermute(x, axis, [(d, d ^ mask) for d in range(count)])


def choose(bit, x):
    h = x.shape[0] // 2
    return jnp.where(bit, x[h:], x[:h]), jnp.where(bit, x[:h], x[h:])


def halve(x, axis, index, mask, count):
    keep, send = choose((index & mask) != 0, x)
    return keep + exchange(send, axis, mask, count)


def double(x, axis, index, mask, count):
    other = exchange(x, axis, mask, count)
    bit = (index & mask) != 0
    return jnp.concatenate([jnp.where(bit, other, x), jnp.where(bit, x, other)], axis=0)


def all_sum(x, axis, index, order, count):
    for mask in order:
        x = halve(x, axis, index, mask, count)
    for mask in order[::-1]:
        x = double(x, axis, index, mask, count)
    return x


def spread(x, axis, index, order, count):
    for mask in order:
        other = lax.ppermute(x, axis, [(d, d + mask) for d in range(0, count, 2 * mask)])
        x = jnp.where((index & (2 * mask - 1)) == mask, other, x)
    return x


def collect(x, count, inner):
    return [x] + [
        lax.ppermute(x, AXES, [(d + e, e) for e in range(inner)]) for d in range(inner, count, inner)
    ]


def collect_last(x, inner):
    return [x] + [lax.ppermute(x, AXES, [(e, 0)]) for e in range(1, inner)]


def scatter(x, axis, index, order, count):
    done = 0
    for mask in order:
        pairs = [(d, d + mask) for d in range(count) if d & done == d]
        h = x.shape[0] // 2
        x = jnp.where((index & mask) != 0, lax.ppermute(x[h:], axis, pairs), x[:h])
        done |= mask
    return x


def bits_reversed(count):
    width = count.bit_length() - 1
    return [sum(((j >> b) & 1) << (width - 1 - b) for b in range(width)) for j in range(count)]


def per_device(front, child_tiles, tile_target, tile_count, probe):
    row_count = lax.axis_size("row")
    col_count = lax.axis_size("col")
    devices = row_count * col_count
    local_rows, local_cols = front.shape
    tile_rows = local_rows // TB
    tile_cols = local_cols // TB
    grid = tile_cols * col_count
    held = child_tiles.shape[0]
    capacity = 2 * max(1, (held + devices - 1) // devices)
    row_index = lax.axis_index("row")
    col_index = lax.axis_index("col")
    device = row_index * col_count + col_index
    half = TB // 2

    homes = (PD + local_rows - 1) // local_rows
    most = max(1, homes * capacity // 2)
    picked = pick(tile_target, tile_count, child_tiles, most, grid)
    inner = min(2, row_count) * col_count
    gathered = jnp.concatenate(collect(picked, devices, inner), axis=0)
    gathered, tile_target = lax.optimization_barrier((gathered, tile_target))
    outgoing = stage(tile_target, tile_count, child_tiles, devices, capacity, grid, tile_rows, tile_cols, col_count)
    gathered = jnp.concatenate(collect_last(gathered, inner), axis=0)
    gathered, outgoing = lax.optimization_barrier((gathered, outgoing))
    label = gathered.reshape(devices, -1, LANES)[:, most * half, :most].astype(jnp.int32).reshape(-1)
    corner = front
    if homes > 1:
        corner = [front[:, :PD]] + [lax.ppermute(front[:, :PD], "row", [(home, 0)]) for home in range(1, homes)]
        corner = jnp.concatenate(corner, axis=0)

    incoming = lax.all_to_all(
        outgoing.reshape(devices, capacity * half + 8, LANES), AXES, split_axis=0, concat_axis=0, tiled=True
    )

    packed = inverse_of_factor(label, device.reshape(1), corner, gathered, most, devices)
    order = masks(devices)
    order = order[:1] + [m for m in order[1:] if m >= col_count] + [m for m in order[1:] if m < col_count]
    part = scatter(packed, AXES, device, order, devices)
    part, incoming = lax.optimization_barrier((part, incoming))
    first = jnp.clip(PD - col_index * local_cols, 0, local_cols).reshape(1)
    landing = incoming[:, capacity * half, :capacity].astype(jnp.int32).reshape(-1)
    product, *panel = assemble(
        landing, first, front, incoming.reshape(-1, LANES), probe, capacity, tile_rows, tile_cols, bits_reversed(col_count)
    )

    share = product.reshape(-1, product.shape[2])
    order = order[::-1]
    sums = masks(col_count)
    panel_order = sums[::-1]
    held = {0: panel}
    ahead = lax.ppermute(panel[0], "col", [(0, panel_order[0])])
    for mask in sums[:-1]:
        share = halve(share, "col", col_index, mask, col_count)
    part = double(part, AXES, device, order[0], devices)
    share, part = lax.optimization_barrier((share, part))
    share = halve(share, "col", col_index, sums[-1], col_count)
    for mask in order[1:-2]:
        part = double(part, AXES, device, mask, devices)
    share, part, *later = lax.optimization_barrier((share, part, *panel[1:]))
    part = double(part, AXES, device, order[-2], devices)
    held[panel_order[0]] = [ahead] + [lax.ppermute(piece, "col", [(0, panel_order[0])]) for piece in later]

    top_order = masks(row_count)[::-1]
    if homes == 1:
        top = spread(share[:PD], "row", row_index, top_order[:1], row_count)
        part = double(part, AXES, device, order[-1], devices)
        top = spread(top, "row", row_index, top_order[1:], row_count)
    else:
        pieces = []
        for home in range(homes):
            rows = min(PD - home * local_rows, local_rows)
            pieces.append(jnp.where(row_index == home, share[:rows], 0.0))
        top = all_sum(jnp.concatenate(pieces, axis=0), "row", row_index, masks(row_count), row_count)
        part = double(part, AXES, device, order[-1], devices)
    inverse = unpack(part)

    for mask in panel_order:
        for d in range(0, col_count, 2 * mask):
            if d + mask not in held:
                held[d + mask] = [lax.ppermute(piece, "col", [(d, d + mask)]) for piece in held[d]]
    panels = [held[d] for d in range(col_count)]

    dot = functools.partial(jnp.dot, precision=lax.Precision.HIGH, preferred_element_type=jnp.float32)
    weights = lax.dot_general(
        inverse, dot(inverse, top), (((0,), (0,)), ((), ())), precision=lax.Precision.HIGH, preferred_element_type=jnp.float32
    )
    width = PD // col_count
    mine = lax.dynamic_slice_in_dim(inverse, col_index * width, width, 0)
    return finish(jnp.stack([col_index, row_index * local_rows]), panels, mine, weights, share)


def solution(mesh):
    return jax.shard_map(
        per_device,
        mesh=mesh,
        in_specs=(
            P("row", "col"),
            P(("row", "col"), None),
            P(("row", "col")),
            P(("row", "col")),
            P("col", None),
        ),
        out_specs=(P("row", "col"), P("row", "col")),
        check_vma=False,
    )
```

```python
import functools

import jax
import jax.numpy as jnp
import numpy as np
from jax import lax
from jax.experimental import pallas as pl
from jax.experimental.pallas import tpu as pltpu
from jax.sharding import PartitionSpec as P

NB = 512
PANELS = 2
PD = NB * PANELS
TB = 64
SLOTS = 32
LANES = 128
NBLK = PD // LANES
PACKED = NBLK * (NBLK + 1) // 2
AXES = ("row", "col")
HIGH = lax.Precision.HIGHEST
MIB = 1 << 20
MIDDLE = 3
PIECES = 4


def block_index(r, c):
    return r * (r + 1) // 2 + c


def left_half(shape):
    return lax.broadcasted_iota(jnp.int32, shape, len(shape) - 1) < TB


def magic(divisor, limit):
    x = np.arange(limit, dtype=np.int64)
    for shift in range(8, 31):
        m = (1 << shift) // divisor + 1
        if m * limit < 1 << 31 and np.array_equal((x * m) >> shift, x // divisor):
            return m, shift
    raise ValueError("no multiplier")


def quotient(x, divisor, limit):
    m, shift = magic(divisor, limit)
    return (x * m) >> shift


def is_live(count_ref, t):
    return t % SLOTS < count_ref[t // SLOTS]


def pick_kernel(
    held, most, grid,
    target_ref, count_ref,
    tiles_ref,
    out_ref,
    flat_ref, pair_ref, label_ref, filled_ref,
):
    half = TB // 2
    side = PD // TB
    filled_ref[0] = 0
    for s in range(most):
        label_ref[s] = -1

    def look(t, carry):
        r = quotient(target_ref[t], grid, grid * grid)
        c = target_ref[t] - r * grid

        @pl.when(is_live(count_ref, t) & (r < side) & (c < side))
        def _():
            left = left_half((half, LANES))
            group = tiles_ref[pl.ds(pl.multiple_of(t // 8 * 8, 8), 8), :]
            row = lax.broadcasted_iota(jnp.int32, group.shape, 0)
            line = jnp.sum(jnp.where(row == t % 8, group, 0.0), axis=0, keepdims=True)
            for k in range(half):
                flat_ref[k : k + 1, :] = line[:, k * LANES : (k + 1) * LANES]
            flat = flat_ref[...]
            turned = pltpu.roll(flat, TB, 1)
            pair_ref[pl.ds(0, half, stride=2), :] = jnp.where(left, flat, turned)
            pair_ref[pl.ds(1, half, stride=2), :] = jnp.where(left, turned, flat)
            natural = pair_ref[...]
            mirrored = natural.T[:TB]
            mirrored = jnp.concatenate([mirrored, mirrored], axis=1)
            swap = r // 2 > c // 2
            value = jnp.where(swap, mirrored, natural) * jnp.where(r // 2 == c // 2, 2.0, 1.0)
            filled = filled_ref[0]
            out_ref[pl.ds(pl.multiple_of(filled * half, half), half), :] = jnp.where(left, value[:half], pltpu.roll(value[half:], TB, 1))
            label_ref[filled] = jnp.where(swap, c * side + r, r * side + c)
            filled_ref[0] = filled + 1

        return carry

    lax.fori_loop(0, held, look, 0)
    lane = lax.broadcasted_iota(jnp.int32, (8, LANES), 1)
    line = jnp.full((8, LANES), -1, jnp.int32)
    for s in range(most):
        line = jnp.where(lane == s, label_ref[s], line)
    out_ref[most * half : most * half + 8, :] = line.astype(jnp.float32)


def pick(target, count, child_tiles, most, grid):
    held = child_tiles.shape[0]
    smem = pl.BlockSpec(memory_space=pltpu.SMEM)
    rows = most * TB // 2 + 8
    return pl.pallas_call(
        functools.partial(pick_kernel, held, most, grid),
        grid=(1,),
        out_shape=jax.ShapeDtypeStruct((rows, LANES), jnp.float32),
        in_specs=[smem] * 2 + [pl.BlockSpec((held, TB * TB), lambda i: (0, 0))],
        out_specs=pl.BlockSpec((rows, LANES), lambda i: (0, 0)),
        scratch_shapes=[
            pltpu.VMEM((TB // 2, LANES), jnp.float32),
            pltpu.VMEM((TB, LANES), jnp.float32),
            pltpu.SMEM((most,), jnp.int32),
            pltpu.SMEM((1,), jnp.int32),
        ],
        compiler_params=pltpu.CompilerParams(vmem_limit_bytes=16 * MIB),
        name="pick",
    )(target, count, child_tiles)


def stage_kernel(
    held, devices, capacity, grid, tile_rows, tile_cols, col_count,
    target_ref, tally_ref,
    tiles_ref,
    out_ref,
    flat_ref, pair_ref, count_ref, slot_ref, landing_ref,
):
    half = TB // 2
    for d in range(devices):
        count_ref[d] = 0

    def clear(s, carry):
        landing_ref[s] = -1
        return carry

    lax.fori_loop(0, devices * capacity, clear, 0)

    def spread_out(g, carry):
        rows = tiles_ref[pl.ds(pl.multiple_of(g * 8, 8), 8), :]
        for k in range(half):
            flat_ref[pl.ds(g * 8 * half + k, 8, stride=half), :] = rows[:, k * LANES : (k + 1) * LANES]
        return carry

    lax.fori_loop(0, held // 8, spread_out, 0)

    def assign(t, carry):
        alive = is_live(tally_ref, t)
        r = quotient(target_ref[t], grid, grid * grid)
        c = target_ref[t] - r * grid
        for m, (a, b) in enumerate(((r, c), (c, r))):
            home = quotient(a, tile_rows, grid)
            side = quotient(b, tile_cols, grid)
            owner = home * col_count + side
            place = (a - home * tile_rows) * tile_cols + (b - side * tile_cols)
            filled = count_ref[owner]
            count_ref[owner] = filled + 1
            slot = owner * capacity + filled
            slot_ref[m * held + t] = owner * (capacity * half + 8) + filled * half
            landing_ref[slot] = jnp.where(alive, place, -1)
        return carry

    lax.fori_loop(0, held, assign, 0, unroll=4)

    def put(index, value):
        out_ref[pl.ds(pl.multiple_of(slot_ref[index], 8), half), :] = value

    def quad(q, carry):
        left = left_half((half, LANES))
        naturals = []
        for p in range(2):
            a = flat_ref[pl.ds(pl.multiple_of((4 * q + 2 * p) * half, half), half), :]
            b = flat_ref[pl.ds(pl.multiple_of((4 * q + 2 * p + 1) * half, half), half), :]
            pair_ref[p, pl.ds(0, half, stride=2), :] = jnp.where(left, a, pltpu.roll(b, TB, 1))
            pair_ref[p, pl.ds(1, half, stride=2), :] = jnp.where(left, pltpu.roll(a, TB, 1), b)
            naturals.append(pair_ref[p, :, :])
        turned = jnp.concatenate(naturals, axis=0).T
        for m, values, order in (
            (0, naturals[0], (0, 1)),
            (0, naturals[1], (2, 3)),
            (1, turned[:TB], (0, 2)),
            (1, turned[TB:], (1, 3)),
        ):
            up, low = values[:half], values[half:]
            put(m * held + 4 * q + order[0], jnp.where(left, up, pltpu.roll(low, TB, 1)))
            put(m * held + 4 * q + order[1], jnp.where(left, pltpu.roll(up, TB, 1), low))
        return carry

    lax.fori_loop(0, held // 4, quad, 0, unroll=2)

    lane = lax.broadcasted_iota(jnp.int32, (8, LANES), 1)

    def label(d, carry):
        line = jnp.full((8, LANES), -1, jnp.int32)
        for s in range(capacity):
            line = jnp.where(lane == s, landing_ref[d * capacity + s], line)
        at = d * (capacity * half + 8) + capacity * half
        out_ref[pl.ds(pl.multiple_of(at, 8), 8), :] = line.astype(jnp.float32)
        return carry

    lax.fori_loop(0, devices, label, 0)


def stage(target, tally, child_tiles, devices, capacity, grid, tile_rows, tile_cols, col_count):
    held = child_tiles.shape[0]
    half = TB // 2
    smem = pl.BlockSpec(memory_space=pltpu.SMEM)
    rows = devices * (capacity * half + 8)
    return pl.pallas_call(
        functools.partial(stage_kernel, held, devices, capacity, grid, tile_rows, tile_cols, col_count),
        grid=(1,),
        out_shape=jax.ShapeDtypeStruct((rows, LANES), jnp.float32),
        in_specs=[smem] * 2 + [pl.BlockSpec((held, TB * TB), lambda i: (0, 0))],
        out_specs=pl.BlockSpec((rows, LANES), lambda i: (0, 0)),
        scratch_shapes=[
            pltpu.VMEM((held * half, LANES), jnp.float32),
            pltpu.VMEM((2, TB, LANES), jnp.float32),
            pltpu.SMEM((devices,), jnp.int32),
            pltpu.SMEM((2 * held,), jnp.int32),
            pltpu.SMEM((devices * capacity,), jnp.int32),
        ],
        compiler_params=pltpu.CompilerParams(vmem_limit_bytes=24 * MIB),
        name="stage",
    )(target, tally, child_tiles)


def split(x):
    high = x.astype(jnp.bfloat16)
    return high, (x - high.astype(jnp.float32)).astype(jnp.bfloat16)


def dot3(left_high, left_low, right_high, right_low):
    dot = functools.partial(jnp.dot, preferred_element_type=jnp.float32)
    return dot(left_high, right_high) + (dot(left_high, right_low) + dot(left_low, right_high))


def lane_splat(x, lane):
    return jnp.broadcast_to(x[:, lane : lane + 1], x.shape)


def row_splat(ref, row):
    return jnp.broadcast_to(ref[row : row + 1, :], (8, LANES))


def inverse_factor(strips, splat_ref):
    strips = list(strips)
    lane = lax.broadcasted_iota(jnp.int32, (8, LANES), 1)
    sub = lax.broadcasted_iota(jnp.int32, (8, LANES), 0)
    result = []
    for k in range(LANES // 8):
        strip = strips[k]
        columns = [lane_splat(strip, 8 * k + t) for t in range(8)]
        for t in range(8):
            splat_ref[8 * t : 8 * t + 8, :] = columns[t]
        e = [[row_splat(splat_ref, 8 * t + s) if s <= t else None for t in range(8)] for s in range(8)]
        low = [[None] * 8 for _ in range(8)]
        inv = [None] * 8
        for s in range(8):
            inv[s] = lax.rsqrt(e[s][s])
            for t in range(s + 1, 8):
                low[t][s] = e[s][t] * inv[s]
            for t in range(s + 1, 8):
                for u in range(t, 8):
                    e[t][u] = e[t][u] - low[t][s] * low[u][s]
        li = [[None] * 8 for _ in range(8)]
        for s in range(8):
            li[s][s] = inv[s]
            for r in range(s + 1, 8):
                total = low[r][s] * li[s][s]
                for q in range(s + 1, r):
                    total = total + low[r][q] * li[q][s]
                li[r][s] = -inv[r] * total
        inside = (lane >= 8 * k) & (lane < 8 * k + 8)
        unit = jnp.where(lane - 8 * k == sub, 1.0, 0.0)
        strip = jnp.where(inside, unit, strip)
        splat_ref[64:72, :] = strip
        rows = [row_splat(splat_ref, 64 + s) for s in range(8)]
        u = []
        for r in range(8):
            total = li[r][0] * rows[0]
            for s in range(1, r + 1):
                total = total + li[r][s] * rows[s]
            u.append(total)
        mine = u[0]
        for r in range(1, 8):
            mine = jnp.where(sub == r, u[r], mine)
        result.append(jnp.where(lane < 8 * k + 8, mine, 0.0))
        if k + 1 == LANES // 8:
            break
        v = []
        for s in range(8):
            total = li[s][s] * u[s]
            for r in range(s + 1, 8):
                total = total + li[r][s] * u[r]
            v.append(total)
        for i in range(k + 1, LANES // 8):
            old = strips[i]
            total = lane_splat(old, 8 * k) * v[0]
            for s in range(1, 8):
                total = total + lane_splat(old, 8 * k + s) * v[s]
            strips[i] = jnp.where(inside, 0.0, old) - total
    return result


def factor_kernel(
    most, senders,
    label_ref, me_ref,
    front_ref, tiles_ref,
    packed_ref,
    out_ref, top_ref, small_ref, high_ref, low_ref, splat_ref, semaphore,
):
    @pl.when(me_ref[0] == 0)
    def _():
        copy = pltpu.make_async_copy(front_ref.at[:PD, :PD], out_ref, semaphore)
        copy.start()
        copy.wait()
        factor(most, senders, label_ref, front_ref, tiles_ref, packed_ref, out_ref, top_ref, small_ref, high_ref, low_ref, splat_ref)


def factor(most, senders, label_ref, front_ref, tiles_ref, packed_ref, out_ref, top_ref, small_ref, high_ref, low_ref, splat_ref):
    half = TB // 2
    side = PD // TB
    for r in range(NBLK):
        rows = slice(r * LANES, (r + 1) * LANES)
        if r > 0:
            out_ref[rows, : r * LANES] = jnp.zeros((LANES, r * LANES), jnp.float32)
    left = left_half((half, LANES))
    group = 8 if most * senders % 8 == 0 else 2

    def place(g, carry):
        parts = []
        for e in range(group):
            s = g * group + e
            p = label_ref[s]
            alive = p >= 0
            p = jnp.clip(p, 0, side * side - 1)
            r, c = p // side, p % side
            even = c % 2 == 0
            source = s // most * (most * half + 8) + s % most * half
            packed = tiles_ref[pl.ds(pl.multiple_of(source, 8), half), :]
            turned = pltpu.roll(packed, TB, 1)
            mask = (left == even) & alive
            top = jnp.where(mask, jnp.where(even, packed, turned), 0.0)
            low = jnp.where(mask, jnp.where(even, turned, packed), 0.0)
            parts.append((r, c // 2, top, low))
        for r, c, top, low in parts:
            cols = pl.ds(pl.multiple_of(c * LANES, LANES), LANES)
            out_ref[pl.ds(pl.multiple_of(r * TB, TB), half), cols] += top
            out_ref[pl.ds(pl.multiple_of(r * TB + half, half), half), cols] += low
        return carry

    lax.fori_loop(0, most * senders // group, place, 0)

    eye = jnp.where(
        lax.broadcasted_iota(jnp.int32, (LANES, LANES), 0) == lax.broadcasted_iota(jnp.int32, (LANES, LANES), 1), 1.0, 0.0
    )

    def outer(k, carry):
        at = pl.multiple_of(k * LANES, LANES)
        here = pl.ds(at, LANES)
        block = out_ref[here, here]
        block = 0.5 * (block + block.T)
        small_ref[...] = block
        strips = inverse_factor([small_ref[8 * i : 8 * i + 8, :] for i in range(LANES // 8)], splat_ref)
        for i, strip in enumerate(strips):
            small_ref[8 * i : 8 * i + 8, :] = strip
        out_ref[here, here] = eye
        top = dot3(*split(small_ref[...]), *split(out_ref[here, :]))
        top_ref[...] = top
        column = lax.broadcasted_iota(jnp.int32, (LANES, PD), 1)
        out_ref[here, :] = jnp.where(column < at + LANES, top, 0.0)
        high_ref[...], low_ref[...] = split(top)
        for step in range(NBLK - 1):

            @pl.when(k == step)
            def _():
                edge = (step + 1) * LANES
                for start in range(edge, PD, LANES):
                    there = slice(start, start + LANES)
                    across = split(top_ref[:, there].T)
                    out_ref[there, :edge] = jnp.where(
                        lax.broadcasted_iota(jnp.int32, (LANES, edge), 1) < edge - LANES, out_ref[there, :edge], 0.0
                    ) - dot3(*across, high_ref[:, :edge], low_ref[:, :edge])
                    out_ref[there, start:] -= dot3(*across, high_ref[:, start:], low_ref[:, start:])

        return carry

    lax.fori_loop(0, NBLK, outer, 0)
    for r in range(NBLK):
        for c in range(r + 1):
            base = block_index(r, c) * LANES
            packed_ref[base : base + LANES, :] = out_ref[r * LANES : (r + 1) * LANES, c * LANES : (c + 1) * LANES]


def inverse_of_factor(label, me, front, tiles, most, senders):
    smem = pl.BlockSpec(memory_space=pltpu.SMEM)
    return pl.pallas_call(
        functools.partial(factor_kernel, most, senders),
        grid=(1,),
        out_shape=jax.ShapeDtypeStruct((PACKED * LANES, LANES), jnp.float32),
        in_specs=[smem, smem, pl.BlockSpec(memory_space=pl.ANY), pl.BlockSpec(tiles.shape, lambda i: (0, 0))],
        out_specs=pl.BlockSpec((PACKED * LANES, LANES), lambda i: (0, 0)),
        scratch_shapes=[
            pltpu.VMEM((PD, PD), jnp.float32),
            pltpu.VMEM((LANES, PD), jnp.float32),
            pltpu.VMEM((LANES, LANES), jnp.float32),
            pltpu.VMEM((LANES, PD), jnp.bfloat16),
            pltpu.VMEM((LANES, PD), jnp.bfloat16),
            pltpu.VMEM((72, LANES), jnp.float32),
            pltpu.SemaphoreType.DMA,
        ],
        compiler_params=pltpu.CompilerParams(vmem_limit_bytes=56 * MIB),
        name="factor",
    )(label, me, front, tiles)


def unpack_kernel(packed_ref, out_ref):
    for r in range(NBLK):
        for c in range(NBLK):
            rows, cols = slice(r * LANES, (r + 1) * LANES), slice(c * LANES, (c + 1) * LANES)
            if c > r:
                out_ref[rows, cols] = jnp.zeros((LANES, LANES), jnp.float32)
            else:
                base = block_index(r, c) * LANES
                out_ref[rows, cols] = packed_ref[base : base + LANES, :]


def unpack(packed):
    vmem = pl.BlockSpec(memory_space=pltpu.VMEM)
    return pl.pallas_call(
        unpack_kernel,
        out_shape=jax.ShapeDtypeStruct((PD, PD), jnp.float32),
        in_specs=[vmem],
        out_specs=vmem,
        compiler_params=pltpu.CompilerParams(vmem_limit_bytes=16 * MIB),
        name="unpack",
    )(packed)


def assemble_kernel(
    slots, capacity, tile_cols, limit, row_chunk, width, order,
    landing_ref, first_ref,
    front_ref, incoming_ref, probe_ref,
    product_ref, *rest,
):
    panels, (matrix_ref, high_ref, low_ref, semaphore) = rest[:-4], rest[-4:]
    copy = pltpu.make_async_copy(front_ref, matrix_ref, semaphore)
    copy.start()
    step = 256 if probe_ref.shape[0] % 256 == 0 else 128
    half = TB // 2

    def cut(s, carry):
        rows = pl.ds(pl.multiple_of(s * step, step), step)
        index = lax.broadcasted_iota(jnp.int32, (step, probe_ref.shape[1]), 0) + s * step
        high, low = split(jnp.where(index >= first_ref[0], probe_ref[rows, :], 0.0))
        high_ref[rows, :] = high
        low_ref[rows, :] = low
        return carry

    lax.fori_loop(0, probe_ref.shape[0] // step, cut, 0)
    copy.wait()
    block = capacity * half + 8
    group = 8 if slots % 8 == 0 else 2
    left = left_half((half, LANES))

    def place(g, carry):
        parts = []
        for e in range(group):
            s = g * group + e
            p = landing_ref[s]
            alive = p >= 0
            p = jnp.maximum(p, 0)
            r = quotient(p, tile_cols, limit)
            c = p - r * tile_cols
            even = c % 2 == 0
            source = s // capacity * block + s % capacity * half
            packed = incoming_ref[pl.ds(pl.multiple_of(source, 8), half), :]
            turned = pltpu.roll(packed, TB, 1)
            mask = (left == even) & alive
            top = jnp.where(mask, jnp.where(even, packed, turned), 0.0)
            low = jnp.where(mask, jnp.where(even, turned, packed), 0.0)
            parts.append((r, c // 2, top, low))
        for r, c, top, low in parts:
            cols = pl.ds(pl.multiple_of(c * LANES, LANES), LANES)
            matrix_ref[pl.ds(pl.multiple_of(r * TB, TB), half), cols] += top
            matrix_ref[pl.ds(pl.multiple_of(r * TB + half, half), half), cols] += low
        return carry

    lax.fori_loop(0, slots // group, place, 0)
    rows = matrix_ref.shape[0] // len(panels)
    for i, panel_ref in enumerate(panels):
        panel_ref[...] = matrix_ref[i * rows : (i + 1) * rows, :PD]

    def multiply(b, carry):
        rows = pl.ds(pl.multiple_of(b * row_chunk, row_chunk), row_chunk)
        high, low = split(matrix_ref[rows, :])
        dot = functools.partial(jnp.dot, preferred_element_type=jnp.float32)
        total = dot(high, high_ref[...]) + (dot(high, low_ref[...]) + dot(low, high_ref[...]))
        for j, at in enumerate(order):
            product_ref[at, rows, :] = total[:, j * width : (j + 1) * width]
        return carry

    lax.fori_loop(0, matrix_ref.shape[0] // row_chunk, multiply, 0)


def assemble(landing, first, front, incoming, probe, capacity, tile_rows, tile_cols, order):
    local_rows, local_cols = front.shape
    columns = probe.shape[1]
    width = columns // len(order)
    smem = pl.BlockSpec(memory_space=pltpu.SMEM)
    vmem = pl.BlockSpec(memory_space=pltpu.VMEM)
    row_chunk = 192 if local_rows % 192 == 0 else 64
    return pl.pallas_call(
        functools.partial(
            assemble_kernel, landing.shape[0], capacity, tile_cols, tile_rows * tile_cols, row_chunk, width, order
        ),
        out_shape=(jax.ShapeDtypeStruct((len(order), local_rows, width), jnp.float32),)
        + (jax.ShapeDtypeStruct((local_rows // PIECES, PD), jnp.float32),) * PIECES,
        in_specs=[smem] * 2 + [pl.BlockSpec(memory_space=pl.ANY), vmem, vmem],
        out_specs=(vmem,) * (1 + PIECES),
        scratch_shapes=[
            pltpu.VMEM((local_rows, local_cols), jnp.float32),
            pltpu.VMEM((local_cols, columns), jnp.bfloat16),
            pltpu.VMEM((local_cols, columns), jnp.bfloat16),
            pltpu.SemaphoreType.DMA,
        ],
        compiler_params=pltpu.CompilerParams(vmem_limit_bytes=56 * MIB),
        name="assemble",
    )(landing, first, front, incoming, probe)


def finish_kernel(
    sources, width,
    where_ref, *refs,
):
    panels = refs[: sources * PIECES]
    inverse_ref, weights_ref, share_ref, solved_ref, sketch_ref, panel_ref, semaphore = refs[sources * PIECES :]
    col, row_start = where_ref[0], where_ref[1]
    piece = panel_ref.shape[0] // PIECES
    for j in range(sources):

        @pl.when(col == j)
        def _():
            moves = [
                pltpu.make_async_copy(panels[j * PIECES + i], panel_ref.at[i * piece : (i + 1) * piece], semaphore.at[i])
                for i in range(PIECES)
            ]
            for move in moves:
                move.start()
            for move in moves:
                move.wait()

    right_high, right_low = split(jnp.concatenate([inverse_ref[...].T, weights_ref[...]], axis=1))
    dot = functools.partial(jnp.dot, preferred_element_type=jnp.float32)
    step = 192 if panel_ref.shape[0] % 192 == 0 else 64

    def body(b, carry):
        rows = pl.ds(pl.multiple_of(b * step, step), step)
        high, low = split(panel_ref[rows, :])
        total = dot(high, right_high) + (dot(high, right_low) + dot(low, right_high))
        index = row_start + b * step + lax.broadcasted_iota(jnp.int32, (step, width), 0)
        column = col * width + lax.broadcasted_iota(jnp.int32, (step, width), 1)
        solved_ref[rows, :] = jnp.where(index >= (column // NB) * NB, total[:, :width], 0.0)
        rest = share_ref[rows, :] - total[:, width:]
        index = row_start + b * step + lax.broadcasted_iota(jnp.int32, rest.shape, 0)
        sketch_ref[rows, :] = jnp.where(index >= PD, rest, 0.0)
        return carry

    lax.fori_loop(0, panel_ref.shape[0] // step, body, 0)


def finish(where, panels, inverse, weights, share):
    local_rows = share.shape[0]
    width = inverse.shape[0]
    vmem = pl.BlockSpec(memory_space=pltpu.VMEM)
    return pl.pallas_call(
        functools.partial(finish_kernel, len(panels), width),
        out_shape=(
            jax.ShapeDtypeStruct((local_rows, width), jnp.float32),
            jax.ShapeDtypeStruct(share.shape, jnp.float32),
        ),
        in_specs=[pl.BlockSpec(memory_space=pltpu.SMEM)] + [pl.BlockSpec(memory_space=pl.ANY)] * (len(panels) * PIECES) + [vmem] * 3,
        out_specs=(vmem, vmem),
        scratch_shapes=[pltpu.VMEM((local_rows, PD), jnp.float32), pltpu.SemaphoreType.DMA((PIECES,))],
        compiler_params=pltpu.CompilerParams(vmem_limit_bytes=28 * MIB),
        name="finish",
    )(where, *sum(panels, []), inverse, weights, share)


def masks(count):
    return [1 << b for b in range(count.bit_length() - 1)]


def exchange(x, axis, mask, count):
    return lax.ppermute(x, axis, [(d, d ^ mask) for d in range(count)])


def choose(bit, x):
    h = x.shape[0] // 2
    return jnp.where(bit, x[h:], x[:h]), jnp.where(bit, x[:h], x[h:])


def halve(x, axis, index, mask, count):
    keep, send = choose((index & mask) != 0, x)
    return keep + exchange(send, axis, mask, count)


def double(x, axis, index, mask, count):
    other = exchange(x, axis, mask, count)
    bit = (index & mask) != 0
    return jnp.concatenate([jnp.where(bit, other, x), jnp.where(bit, x, other)], axis=0)


def all_sum(x, axis, index, order, count):
    for mask in order:
        x = halve(x, axis, index, mask, count)
    for mask in order[::-1]:
        x = double(x, axis, index, mask, count)
    return x


def spread(x, axis, index, order, count):
    for mask in order:
        other = lax.ppermute(x, axis, [(d, d + mask) for d in range(0, count, 2 * mask)])
        x = jnp.where((index & (2 * mask - 1)) == mask, other, x)
    return x


def collect(x, count, inner, pair):
    heads = range(0, inner, pair)
    offsets = [far + near for far in range(0, count, inner) for near in range(pair) if far + near > 0]
    return [x] + [lax.ppermute(x, AXES, [(e + offset, e) for e in heads]) for offset in offsets]


def collect_last(x, inner, pair):
    return [x] + [lax.ppermute(x, AXES, [(e, 0)]) for e in range(pair, inner, pair)]


def scatter(x, axis, index, order, count):
    done = 0
    for mask in order:
        pairs = [(d, d + mask) for d in range(count) if d & done == d]
        h = x.shape[0] // 2
        x = jnp.where((index & mask) != 0, lax.ppermute(x[h:], axis, pairs), x[:h])
        done |= mask
    return x


def bits_reversed(count):
    width = count.bit_length() - 1
    return [sum(((j >> b) & 1) << (width - 1 - b) for b in range(width)) for j in range(count)]


def per_device(front, child_tiles, tile_target, tile_count, probe):
    row_count = lax.axis_size("row")
    col_count = lax.axis_size("col")
    devices = row_count * col_count
    local_rows, local_cols = front.shape
    tile_rows = local_rows // TB
    tile_cols = local_cols // TB
    grid = tile_cols * col_count
    held = child_tiles.shape[0]
    capacity = 2 * max(1, (held + devices - 1) // devices)
    row_index = lax.axis_index("row")
    col_index = lax.axis_index("col")
    device = row_index * col_count + col_index
    half = TB // 2

    homes = (PD + local_rows - 1) // local_rows
    most = max(1, homes * capacity // 2)
    picked = pick(tile_target, tile_count, child_tiles, most, grid)
    inner, pair = min(2, row_count) * col_count, min(2, col_count)
    gathered = jnp.concatenate(collect(picked, devices, inner, pair), axis=0)
    gathered, tile_target = lax.optimization_barrier((gathered, tile_target))
    outgoing = stage(tile_target, tile_count, child_tiles, devices, capacity, grid, tile_rows, tile_cols, col_count)
    gathered = jnp.concatenate(collect_last(gathered, inner, pair), axis=0)
    gathered, outgoing = lax.optimization_barrier((gathered, outgoing))
    label = gathered.reshape(devices, -1, LANES)[:, most * half, :most].astype(jnp.int32).reshape(-1)
    corner = front
    if homes > 1:
        corner = [front[:, :PD]] + [lax.ppermute(front[:, :PD], "row", [(home, 0)]) for home in range(1, homes)]
        corner = jnp.concatenate(corner, axis=0)

    incoming = lax.all_to_all(
        outgoing.reshape(devices, capacity * half + 8, LANES), AXES, split_axis=0, concat_axis=0, tiled=True
    )

    packed = inverse_of_factor(label, device.reshape(1), corner, gathered, most, devices)
    order = masks(devices)
    order = order[:1] + [m for m in order[1:] if m >= col_count] + [m for m in order[1:] if m < col_count]
    part = scatter(packed, AXES, device, order, devices)
    part, incoming = lax.optimization_barrier((part, incoming))
    first = jnp.clip(PD - col_index * local_cols, 0, local_cols).reshape(1)
    landing = incoming[:, capacity * half, :capacity].astype(jnp.int32).reshape(-1)
    product, *panel = assemble(
        landing, first, front, incoming.reshape(-1, LANES), probe, capacity, tile_rows, tile_cols, bits_reversed(col_count)
    )

    share = product.reshape(-1, product.shape[2])
    order = order[::-1]
    sums = masks(col_count)
    panel_order = sums[::-1]
    far = [(0, panel_order[0])]
    sent = [lax.ppermute(panel[0], "col", far)]
    for mask in sums[:-1]:
        share = halve(share, "col", col_index, mask, col_count)
    part = double(part, AXES, device, order[0], devices)
    share, part, *panel[1:] = lax.optimization_barrier((share, part, *panel[1:]))
    sent += [lax.ppermute(piece, "col", far) for piece in panel[1:MIDDLE]]
    share = halve(share, "col", col_index, sums[-1], col_count)
    for mask in order[1:-2]:
        part = double(part, AXES, device, mask, devices)
    share, part, *panel[MIDDLE:] = lax.optimization_barrier((share, part, *panel[MIDDLE:]))
    sent += [lax.ppermute(piece, "col", far) for piece in panel[MIDDLE:]]
    part = double(part, AXES, device, order[-2], devices)
    held = {0: panel, panel_order[0]: sent}

    top_order = masks(row_count)[::-1]
    if homes == 1:
        top = spread(share[:PD], "row", row_index, top_order[:1], row_count)
        part = double(part, AXES, device, order[-1], devices)
        top = spread(top, "row", row_index, top_order[1:], row_count)
    else:
        pieces = []
        for home in range(homes):
            rows = min(PD - home * local_rows, local_rows)
            pieces.append(jnp.where(row_index == home, share[:rows], 0.0))
        top = all_sum(jnp.concatenate(pieces, axis=0), "row", row_index, masks(row_count), row_count)
        part = double(part, AXES, device, order[-1], devices)
    inverse = unpack(part)

    for mask in panel_order:
        for d in range(0, col_count, 2 * mask):
            if d + mask not in held:
                held[d + mask] = [lax.ppermute(piece, "col", [(d, d + mask)]) for piece in held[d]]
    panels = [held[d] for d in range(col_count)]

    dot = functools.partial(jnp.dot, precision=lax.Precision.HIGH, preferred_element_type=jnp.float32)
    weights = lax.dot_general(
        inverse, dot(inverse, top), (((0,), (0,)), ((), ())), precision=lax.Precision.HIGH, preferred_element_type=jnp.float32
    )
    width = PD // col_count
    mine = lax.dynamic_slice_in_dim(inverse, col_index * width, width, 0)
    return finish(jnp.stack([col_index, row_index * local_rows]), panels, mine, weights, share)


def solution(mesh):
    return jax.shard_map(
        per_device,
        mesh=mesh,
        in_specs=(
            P("row", "col"),
            P(("row", "col"), None),
            P(("row", "col")),
            P(("row", "col")),
            P("col", None),
        ),
        out_specs=(P("row", "col"), P("row", "col")),
        check_vma=False,
    )
```

```python
import functools

import jax
import jax.numpy as jnp
import numpy as np
from jax import lax
from jax.experimental import pallas as pl
from jax.experimental.pallas import tpu as pltpu
from jax.sharding import PartitionSpec as P

NB = 512
PANELS = 2
PD = NB * PANELS
TB = 64
SLOTS = 32
LANES = 128
NBLK = PD // LANES
PACKED = NBLK * (NBLK + 1) // 2
AXES = ("row", "col")
HIGH = lax.Precision.HIGHEST
MIB = 1 << 20
MIDDLE = 3
PIECES = 4


def block_index(r, c):
    return r * (r + 1) // 2 + c


def left_half(shape):
    return lax.broadcasted_iota(jnp.int32, shape, len(shape) - 1) < TB


def magic(divisor, limit):
    x = np.arange(limit, dtype=np.int64)
    for shift in range(8, 31):
        m = (1 << shift) // divisor + 1
        if m * limit < 1 << 31 and np.array_equal((x * m) >> shift, x // divisor):
            return m, shift
    raise ValueError("no multiplier")


def quotient(x, divisor, limit):
    m, shift = magic(divisor, limit)
    return (x * m) >> shift


def is_live(count_ref, t):
    return t % SLOTS < count_ref[t // SLOTS]


def pick_kernel(
    held, most, grid,
    target_ref, count_ref,
    tiles_ref,
    out_ref,
    flat_ref, pair_ref, label_ref, filled_ref,
):
    half = TB // 2
    side = PD // TB
    filled_ref[0] = 0
    for s in range(most):
        label_ref[s] = -1

    def look(t, carry):
        r = quotient(target_ref[t], grid, grid * grid)
        c = target_ref[t] - r * grid

        @pl.when(is_live(count_ref, t) & (r < side) & (c < side))
        def _():
            left = left_half((half, LANES))
            group = tiles_ref[pl.ds(pl.multiple_of(t // 8 * 8, 8), 8), :]
            row = lax.broadcasted_iota(jnp.int32, group.shape, 0)
            line = jnp.sum(jnp.where(row == t % 8, group, 0.0), axis=0, keepdims=True)
            for k in range(half):
                flat_ref[k : k + 1, :] = line[:, k * LANES : (k + 1) * LANES]
            flat = flat_ref[...]
            turned = pltpu.roll(flat, TB, 1)
            pair_ref[pl.ds(0, half, stride=2), :] = jnp.where(left, flat, turned)
            pair_ref[pl.ds(1, half, stride=2), :] = jnp.where(left, turned, flat)
            natural = pair_ref[...]
            mirrored = natural.T[:TB]
            mirrored = jnp.concatenate([mirrored, mirrored], axis=1)
            swap = r // 2 > c // 2
            value = jnp.where(swap, mirrored, natural) * jnp.where(r // 2 == c // 2, 2.0, 1.0)
            filled = filled_ref[0]
            out_ref[pl.ds(pl.multiple_of(filled * half, half), half), :] = jnp.where(left, value[:half], pltpu.roll(value[half:], TB, 1))
            label_ref[filled] = jnp.where(swap, c * side + r, r * side + c)
            filled_ref[0] = filled + 1

        return carry

    lax.fori_loop(0, held, look, 0, unroll=4)
    lane = lax.broadcasted_iota(jnp.int32, (8, LANES), 1)
    line = jnp.full((8, LANES), -1, jnp.int32)
    for s in range(most):
        line = jnp.where(lane == s, label_ref[s], line)
    out_ref[most * half : most * half + 8, :] = line.astype(jnp.float32)


def pick(target, count, child_tiles, most, grid):
    held = child_tiles.shape[0]
    smem = pl.BlockSpec(memory_space=pltpu.SMEM)
    rows = most * TB // 2 + 8
    return pl.pallas_call(
        functools.partial(pick_kernel, held, most, grid),
        grid=(1,),
        out_shape=jax.ShapeDtypeStruct((rows, LANES), jnp.float32),
        in_specs=[smem] * 2 + [pl.BlockSpec((held, TB * TB), lambda i: (0, 0))],
        out_specs=pl.BlockSpec((rows, LANES), lambda i: (0, 0)),
        scratch_shapes=[
            pltpu.VMEM((TB // 2, LANES), jnp.float32),
            pltpu.VMEM((TB, LANES), jnp.float32),
            pltpu.SMEM((most,), jnp.int32),
            pltpu.SMEM((1,), jnp.int32),
        ],
        compiler_params=pltpu.CompilerParams(vmem_limit_bytes=16 * MIB),
        name="pick",
    )(target, count, child_tiles)


def stage_kernel(
    held, devices, capacity, grid, tile_rows, tile_cols, col_count,
    target_ref, tally_ref,
    tiles_ref,
    out_ref,
    flat_ref, pair_ref, count_ref, slot_ref, landing_ref,
):
    half = TB // 2
    for d in range(devices):
        count_ref[d] = 0

    def clear(s, carry):
        landing_ref[s] = -1
        return carry

    lax.fori_loop(0, devices * capacity, clear, 0)

    def spread_out(g, carry):
        rows = tiles_ref[pl.ds(pl.multiple_of(g * 8, 8), 8), :]
        for k in range(half):
            flat_ref[pl.ds(g * 8 * half + k, 8, stride=half), :] = rows[:, k * LANES : (k + 1) * LANES]
        return carry

    lax.fori_loop(0, held // 8, spread_out, 0, unroll=2)

    def assign(t, carry):
        alive = is_live(tally_ref, t)
        r = quotient(target_ref[t], grid, grid * grid)
        c = target_ref[t] - r * grid
        for m, (a, b) in enumerate(((r, c), (c, r))):
            home = quotient(a, tile_rows, grid)
            side = quotient(b, tile_cols, grid)
            owner = home * col_count + side
            place = (a - home * tile_rows) * tile_cols + (b - side * tile_cols)
            filled = count_ref[owner]
            count_ref[owner] = filled + 1
            slot = owner * capacity + filled
            slot_ref[m * held + t] = owner * (capacity * half + 8) + filled * half
            landing_ref[slot] = jnp.where(alive, place, -1)
        return carry

    lax.fori_loop(0, held, assign, 0, unroll=4)

    def put(index, value):
        out_ref[pl.ds(pl.multiple_of(slot_ref[index], 8), half), :] = value

    def quad(q, carry):
        left = left_half((half, LANES))
        naturals = []
        for p in range(2):
            a = flat_ref[pl.ds(pl.multiple_of((4 * q + 2 * p) * half, half), half), :]
            b = flat_ref[pl.ds(pl.multiple_of((4 * q + 2 * p + 1) * half, half), half), :]
            pair_ref[p, pl.ds(0, half, stride=2), :] = jnp.where(left, a, pltpu.roll(b, TB, 1))
            pair_ref[p, pl.ds(1, half, stride=2), :] = jnp.where(left, pltpu.roll(a, TB, 1), b)
            naturals.append(pair_ref[p, :, :])
        turned = jnp.concatenate(naturals, axis=0).T
        for m, values, order in (
            (0, naturals[0], (0, 1)),
            (0, naturals[1], (2, 3)),
            (1, turned[:TB], (0, 2)),
            (1, turned[TB:], (1, 3)),
        ):
            up, low = values[:half], values[half:]
            put(m * held + 4 * q + order[0], jnp.where(left, up, pltpu.roll(low, TB, 1)))
            put(m * held + 4 * q + order[1], jnp.where(left, pltpu.roll(up, TB, 1), low))
        return carry

    lax.fori_loop(0, held // 4, quad, 0, unroll=4)

    lane = lax.broadcasted_iota(jnp.int32, (8, LANES), 1)

    def label(d, carry):
        line = jnp.full((8, LANES), -1, jnp.int32)
        for s in range(capacity):
            line = jnp.where(lane == s, landing_ref[d * capacity + s], line)
        at = d * (capacity * half + 8) + capacity * half
        out_ref[pl.ds(pl.multiple_of(at, 8), 8), :] = line.astype(jnp.float32)
        return carry

    lax.fori_loop(0, devices, label, 0)


def stage(target, tally, child_tiles, devices, capacity, grid, tile_rows, tile_cols, col_count):
    held = child_tiles.shape[0]
    half = TB // 2
    smem = pl.BlockSpec(memory_space=pltpu.SMEM)
    rows = devices * (capacity * half + 8)
    return pl.pallas_call(
        functools.partial(stage_kernel, held, devices, capacity, grid, tile_rows, tile_cols, col_count),
        grid=(1,),
        out_shape=jax.ShapeDtypeStruct((rows, LANES), jnp.float32),
        in_specs=[smem] * 2 + [pl.BlockSpec((held, TB * TB), lambda i: (0, 0))],
        out_specs=pl.BlockSpec((rows, LANES), lambda i: (0, 0)),
        scratch_shapes=[
            pltpu.VMEM((held * half, LANES), jnp.float32),
            pltpu.VMEM((2, TB, LANES), jnp.float32),
            pltpu.SMEM((devices,), jnp.int32),
            pltpu.SMEM((2 * held,), jnp.int32),
            pltpu.SMEM((devices * capacity,), jnp.int32),
        ],
        compiler_params=pltpu.CompilerParams(vmem_limit_bytes=24 * MIB),
        name="stage",
    )(target, tally, child_tiles)


def split(x):
    high = x.astype(jnp.bfloat16)
    return high, (x - high.astype(jnp.float32)).astype(jnp.bfloat16)


def dot3(left_high, left_low, right_high, right_low):
    dot = functools.partial(jnp.dot, preferred_element_type=jnp.float32)
    return dot(left_high, right_high) + (dot(left_high, right_low) + dot(left_low, right_high))


def lane_splat(x, lane):
    return jnp.broadcast_to(x[:, lane : lane + 1], x.shape)


def row_splat(ref, row):
    return jnp.broadcast_to(ref[row : row + 1, :], (8, LANES))


def inverse_factor(strips, splat_ref):
    strips = list(strips)
    lane = lax.broadcasted_iota(jnp.int32, (8, LANES), 1)
    sub = lax.broadcasted_iota(jnp.int32, (8, LANES), 0)
    result = []
    for k in range(LANES // 8):
        strip = strips[k]
        columns = [lane_splat(strip, 8 * k + t) for t in range(8)]
        for t in range(8):
            splat_ref[8 * t : 8 * t + 8, :] = columns[t]
        e = [[row_splat(splat_ref, 8 * t + s) if s <= t else None for t in range(8)] for s in range(8)]
        low = [[None] * 8 for _ in range(8)]
        inv = [None] * 8
        for s in range(8):
            inv[s] = lax.rsqrt(e[s][s])
            for t in range(s + 1, 8):
                low[t][s] = e[s][t] * inv[s]
            for t in range(s + 1, 8):
                for u in range(t, 8):
                    e[t][u] = e[t][u] - low[t][s] * low[u][s]
        li = [[None] * 8 for _ in range(8)]
        for s in range(8):
            li[s][s] = inv[s]
            for r in range(s + 1, 8):
                total = low[r][s] * li[s][s]
                for q in range(s + 1, r):
                    total = total + low[r][q] * li[q][s]
                li[r][s] = -inv[r] * total
        inside = (lane >= 8 * k) & (lane < 8 * k + 8)
        unit = jnp.where(lane - 8 * k == sub, 1.0, 0.0)
        strip = jnp.where(inside, unit, strip)
        splat_ref[64:72, :] = strip
        rows = [row_splat(splat_ref, 64 + s) for s in range(8)]
        u = []
        for r in range(8):
            total = li[r][0] * rows[0]
            for s in range(1, r + 1):
                total = total + li[r][s] * rows[s]
            u.append(total)
        mine = u[0]
        for r in range(1, 8):
            mine = jnp.where(sub == r, u[r], mine)
        result.append(jnp.where(lane < 8 * k + 8, mine, 0.0))
        if k + 1 == LANES // 8:
            break
        v = []
        for s in range(8):
            total = li[s][s] * u[s]
            for r in range(s + 1, 8):
                total = total + li[r][s] * u[r]
            v.append(total)
        for i in range(k + 1, LANES // 8):
            old = strips[i]
            total = lane_splat(old, 8 * k) * v[0]
            for s in range(1, 8):
                total = total + lane_splat(old, 8 * k + s) * v[s]
            strips[i] = jnp.where(inside, 0.0, old) - total
    return result


def factor_kernel(
    most, senders,
    label_ref, me_ref,
    front_ref, tiles_ref,
    packed_ref,
    out_ref, top_ref, small_ref, high_ref, low_ref, splat_ref, semaphore,
):
    @pl.when(me_ref[0] == 0)
    def _():
        copy = pltpu.make_async_copy(front_ref.at[:PD, :PD], out_ref, semaphore)
        copy.start()
        copy.wait()
        factor(most, senders, label_ref, front_ref, tiles_ref, packed_ref, out_ref, top_ref, small_ref, high_ref, low_ref, splat_ref)


def factor(most, senders, label_ref, front_ref, tiles_ref, packed_ref, out_ref, top_ref, small_ref, high_ref, low_ref, splat_ref):
    half = TB // 2
    side = PD // TB
    for r in range(NBLK):
        rows = slice(r * LANES, (r + 1) * LANES)
        if r > 0:
            out_ref[rows, : r * LANES] = jnp.zeros((LANES, r * LANES), jnp.float32)
    left = left_half((half, LANES))
    group = 8 if most * senders % 8 == 0 else 2

    def place(g, carry):
        parts = []
        for e in range(group):
            s = g * group + e
            p = label_ref[s]
            alive = p >= 0
            p = jnp.clip(p, 0, side * side - 1)
            r, c = p // side, p % side
            even = c % 2 == 0
            source = s // most * (most * half + 8) + s % most * half
            packed = tiles_ref[pl.ds(pl.multiple_of(source, 8), half), :]
            turned = pltpu.roll(packed, TB, 1)
            mask = (left == even) & alive
            top = jnp.where(mask, jnp.where(even, packed, turned), 0.0)
            low = jnp.where(mask, jnp.where(even, turned, packed), 0.0)
            parts.append((r, c // 2, top, low))
        for r, c, top, low in parts:
            cols = pl.ds(pl.multiple_of(c * LANES, LANES), LANES)
            out_ref[pl.ds(pl.multiple_of(r * TB, TB), half), cols] += top
            out_ref[pl.ds(pl.multiple_of(r * TB + half, half), half), cols] += low
        return carry

    lax.fori_loop(0, most * senders // group, place, 0)

    eye = jnp.where(
        lax.broadcasted_iota(jnp.int32, (LANES, LANES), 0) == lax.broadcasted_iota(jnp.int32, (LANES, LANES), 1), 1.0, 0.0
    )

    def outer(k, carry):
        at = pl.multiple_of(k * LANES, LANES)
        here = pl.ds(at, LANES)
        block = out_ref[here, here]
        block = 0.5 * (block + block.T)
        small_ref[...] = block
        strips = inverse_factor([small_ref[8 * i : 8 * i + 8, :] for i in range(LANES // 8)], splat_ref)
        for i, strip in enumerate(strips):
            small_ref[8 * i : 8 * i + 8, :] = strip
        out_ref[here, here] = eye
        top = dot3(*split(small_ref[...]), *split(out_ref[here, :]))
        top_ref[...] = top
        column = lax.broadcasted_iota(jnp.int32, (LANES, PD), 1)
        out_ref[here, :] = jnp.where(column < at + LANES, top, 0.0)
        high_ref[...], low_ref[...] = split(top)
        for step in range(NBLK - 1):

            @pl.when(k == step)
            def _():
                edge = (step + 1) * LANES
                for start in range(edge, PD, LANES):
                    there = slice(start, start + LANES)
                    across = split(top_ref[:, there].T)
                    out_ref[there, :edge] = jnp.where(
                        lax.broadcasted_iota(jnp.int32, (LANES, edge), 1) < edge - LANES, out_ref[there, :edge], 0.0
                    ) - dot3(*across, high_ref[:, :edge], low_ref[:, :edge])
                    out_ref[there, start:] -= dot3(*across, high_ref[:, start:], low_ref[:, start:])

        return carry

    lax.fori_loop(0, NBLK, outer, 0)
    for r in range(NBLK):
        for c in range(r + 1):
            base = block_index(r, c) * LANES
            packed_ref[base : base + LANES, :] = out_ref[r * LANES : (r + 1) * LANES, c * LANES : (c + 1) * LANES]


def inverse_of_factor(label, me, front, tiles, most, senders):
    smem = pl.BlockSpec(memory_space=pltpu.SMEM)
    return pl.pallas_call(
        functools.partial(factor_kernel, most, senders),
        grid=(1,),
        out_shape=jax.ShapeDtypeStruct((PACKED * LANES, LANES), jnp.float32),
        in_specs=[smem, smem, pl.BlockSpec(memory_space=pl.ANY), pl.BlockSpec(tiles.shape, lambda i: (0, 0))],
        out_specs=pl.BlockSpec((PACKED * LANES, LANES), lambda i: (0, 0)),
        scratch_shapes=[
            pltpu.VMEM((PD, PD), jnp.float32),
            pltpu.VMEM((LANES, PD), jnp.float32),
            pltpu.VMEM((LANES, LANES), jnp.float32),
            pltpu.VMEM((LANES, PD), jnp.bfloat16),
            pltpu.VMEM((LANES, PD), jnp.bfloat16),
            pltpu.VMEM((72, LANES), jnp.float32),
            pltpu.SemaphoreType.DMA,
        ],
        compiler_params=pltpu.CompilerParams(vmem_limit_bytes=56 * MIB),
        name="factor",
    )(label, me, front, tiles)


def unpack_kernel(packed_ref, out_ref):
    for r in range(NBLK):
        for c in range(NBLK):
            rows, cols = slice(r * LANES, (r + 1) * LANES), slice(c * LANES, (c + 1) * LANES)
            if c > r:
                out_ref[rows, cols] = jnp.zeros((LANES, LANES), jnp.float32)
            else:
                base = block_index(r, c) * LANES
                out_ref[rows, cols] = packed_ref[base : base + LANES, :]


def unpack(packed):
    vmem = pl.BlockSpec(memory_space=pltpu.VMEM)
    return pl.pallas_call(
        unpack_kernel,
        out_shape=jax.ShapeDtypeStruct((PD, PD), jnp.float32),
        in_specs=[vmem],
        out_specs=vmem,
        compiler_params=pltpu.CompilerParams(vmem_limit_bytes=16 * MIB),
        name="unpack",
    )(packed)


def assemble_kernel(
    slots, capacity, tile_cols, limit, row_chunk, width, order,
    landing_ref, first_ref,
    front_ref, incoming_ref, probe_ref,
    product_ref, *rest,
):
    panels, (matrix_ref, high_ref, low_ref, semaphore) = rest[:-4], rest[-4:]
    copy = pltpu.make_async_copy(front_ref, matrix_ref, semaphore)
    copy.start()
    step = 256 if probe_ref.shape[0] % 256 == 0 else 128
    half = TB // 2

    def cut(s, carry):
        rows = pl.ds(pl.multiple_of(s * step, step), step)
        index = lax.broadcasted_iota(jnp.int32, (step, probe_ref.shape[1]), 0) + s * step
        high, low = split(jnp.where(index >= first_ref[0], probe_ref[rows, :], 0.0))
        high_ref[rows, :] = high
        low_ref[rows, :] = low
        return carry

    lax.fori_loop(0, probe_ref.shape[0] // step, cut, 0)
    copy.wait()
    block = capacity * half + 8
    group = 8 if slots % 8 == 0 else 2
    left = left_half((half, LANES))

    def place(g, carry):
        parts = []
        for e in range(group):
            s = g * group + e
            p = landing_ref[s]
            alive = p >= 0
            p = jnp.maximum(p, 0)
            r = quotient(p, tile_cols, limit)
            c = p - r * tile_cols
            even = c % 2 == 0
            source = s // capacity * block + s % capacity * half
            packed = incoming_ref[pl.ds(pl.multiple_of(source, 8), half), :]
            turned = pltpu.roll(packed, TB, 1)
            mask = (left == even) & alive
            top = jnp.where(mask, jnp.where(even, packed, turned), 0.0)
            low = jnp.where(mask, jnp.where(even, turned, packed), 0.0)
            parts.append((r, c // 2, top, low))
        for r, c, top, low in parts:
            cols = pl.ds(pl.multiple_of(c * LANES, LANES), LANES)
            matrix_ref[pl.ds(pl.multiple_of(r * TB, TB), half), cols] += top
            matrix_ref[pl.ds(pl.multiple_of(r * TB + half, half), half), cols] += low
        return carry

    lax.fori_loop(0, slots // group, place, 0)
    rows = matrix_ref.shape[0] // len(panels)
    for i, panel_ref in enumerate(panels):
        panel_ref[...] = matrix_ref[i * rows : (i + 1) * rows, :PD]

    def multiply(b, carry):
        rows = pl.ds(pl.multiple_of(b * row_chunk, row_chunk), row_chunk)
        high, low = split(matrix_ref[rows, :])
        dot = functools.partial(jnp.dot, preferred_element_type=jnp.float32)
        total = dot(high, high_ref[...]) + (dot(high, low_ref[...]) + dot(low, high_ref[...]))
        for j, at in enumerate(order):
            product_ref[at, rows, :] = total[:, j * width : (j + 1) * width]
        return carry

    lax.fori_loop(0, matrix_ref.shape[0] // row_chunk, multiply, 0)


def assemble(landing, first, front, incoming, probe, capacity, tile_rows, tile_cols, order):
    local_rows, local_cols = front.shape
    columns = probe.shape[1]
    width = columns // len(order)
    smem = pl.BlockSpec(memory_space=pltpu.SMEM)
    vmem = pl.BlockSpec(memory_space=pltpu.VMEM)
    row_chunk = 192 if local_rows % 192 == 0 else 64
    return pl.pallas_call(
        functools.partial(
            assemble_kernel, landing.shape[0], capacity, tile_cols, tile_rows * tile_cols, row_chunk, width, order
        ),
        out_shape=(jax.ShapeDtypeStruct((len(order), local_rows, width), jnp.float32),)
        + (jax.ShapeDtypeStruct((local_rows // PIECES, PD), jnp.float32),) * PIECES,
        in_specs=[smem] * 2 + [pl.BlockSpec(memory_space=pl.ANY), vmem, vmem],
        out_specs=(vmem,) * (1 + PIECES),
        scratch_shapes=[
            pltpu.VMEM((local_rows, local_cols), jnp.float32),
            pltpu.VMEM((local_cols, columns), jnp.bfloat16),
            pltpu.VMEM((local_cols, columns), jnp.bfloat16),
            pltpu.SemaphoreType.DMA,
        ],
        compiler_params=pltpu.CompilerParams(vmem_limit_bytes=56 * MIB),
        name="assemble",
    )(landing, first, front, incoming, probe)


def finish_kernel(
    sources, width,
    where_ref, *refs,
):
    panels = refs[: sources * PIECES]
    inverse_ref, weights_ref, share_ref, solved_ref, sketch_ref, panel_ref, semaphore = refs[sources * PIECES :]
    col, row_start = where_ref[0], where_ref[1]
    piece = panel_ref.shape[0] // PIECES
    for j in range(sources):

        @pl.when(col == j)
        def _():
            moves = [
                pltpu.make_async_copy(panels[j * PIECES + i], panel_ref.at[i * piece : (i + 1) * piece], semaphore.at[i])
                for i in range(PIECES)
            ]
            for move in moves:
                move.start()
            for move in moves:
                move.wait()

    right_high, right_low = split(jnp.concatenate([inverse_ref[...].T, weights_ref[...]], axis=1))
    dot = functools.partial(jnp.dot, preferred_element_type=jnp.float32)
    step = 192 if panel_ref.shape[0] % 192 == 0 else 64

    def body(b, carry):
        rows = pl.ds(pl.multiple_of(b * step, step), step)
        high, low = split(panel_ref[rows, :])
        total = dot(high, right_high) + (dot(high, right_low) + dot(low, right_high))
        index = row_start + b * step + lax.broadcasted_iota(jnp.int32, (step, width), 0)
        column = col * width + lax.broadcasted_iota(jnp.int32, (step, width), 1)
        solved_ref[rows, :] = jnp.where(index >= (column // NB) * NB, total[:, :width], 0.0)
        rest = share_ref[rows, :] - total[:, width:]
        index = row_start + b * step + lax.broadcasted_iota(jnp.int32, rest.shape, 0)
        sketch_ref[rows, :] = jnp.where(index >= PD, rest, 0.0)
        return carry

    lax.fori_loop(0, panel_ref.shape[0] // step, body, 0)


def finish(where, panels, inverse, weights, share):
    local_rows = share.shape[0]
    width = inverse.shape[0]
    vmem = pl.BlockSpec(memory_space=pltpu.VMEM)
    return pl.pallas_call(
        functools.partial(finish_kernel, len(panels), width),
        out_shape=(
            jax.ShapeDtypeStruct((local_rows, width), jnp.float32),
            jax.ShapeDtypeStruct(share.shape, jnp.float32),
        ),
        in_specs=[pl.BlockSpec(memory_space=pltpu.SMEM)] + [pl.BlockSpec(memory_space=pl.ANY)] * (len(panels) * PIECES) + [vmem] * 3,
        out_specs=(vmem, vmem),
        scratch_shapes=[pltpu.VMEM((local_rows, PD), jnp.float32), pltpu.SemaphoreType.DMA((PIECES,))],
        compiler_params=pltpu.CompilerParams(vmem_limit_bytes=28 * MIB),
        name="finish",
    )(where, *sum(panels, []), inverse, weights, share)


def masks(count):
    return [1 << b for b in range(count.bit_length() - 1)]


def exchange(x, axis, mask, count):
    return lax.ppermute(x, axis, [(d, d ^ mask) for d in range(count)])


def choose(bit, x):
    h = x.shape[0] // 2
    return jnp.where(bit, x[h:], x[:h]), jnp.where(bit, x[:h], x[h:])


def halve(x, axis, index, mask, count):
    keep, send = choose((index & mask) != 0, x)
    return keep + exchange(send, axis, mask, count)


def double(x, axis, index, mask, count):
    other = exchange(x, axis, mask, count)
    bit = (index & mask) != 0
    return jnp.concatenate([jnp.where(bit, other, x), jnp.where(bit, x, other)], axis=0)


def all_sum(x, axis, index, order, count):
    for mask in order:
        x = halve(x, axis, index, mask, count)
    for mask in order[::-1]:
        x = double(x, axis, index, mask, count)
    return x


def spread(x, axis, index, order, count):
    for mask in order:
        other = lax.ppermute(x, axis, [(d, d + mask) for d in range(0, count, 2 * mask)])
        x = jnp.where((index & (2 * mask - 1)) == mask, other, x)
    return x


def collect(x, count, inner, pair):
    heads = range(0, inner, pair)
    offsets = [far + near for far in range(0, count, inner) for near in range(pair) if far + near > 0]
    return [x] + [lax.ppermute(x, AXES, [(e + offset, e) for e in heads]) for offset in offsets]


def collect_last(x, inner, pair):
    return [x] + [lax.ppermute(x, AXES, [(e, 0)]) for e in range(pair, inner, pair)]


def scatter(x, axis, index, order, count):
    done = 0
    for mask in order:
        pairs = [(d, d + mask) for d in range(count) if d & done == d]
        h = x.shape[0] // 2
        x = jnp.where((index & mask) != 0, lax.ppermute(x[h:], axis, pairs), x[:h])
        done |= mask
    return x


def bits_reversed(count):
    width = count.bit_length() - 1
    return [sum(((j >> b) & 1) << (width - 1 - b) for b in range(width)) for j in range(count)]


def per_device(front, child_tiles, tile_target, tile_count, probe):
    row_count = lax.axis_size("row")
    col_count = lax.axis_size("col")
    devices = row_count * col_count
    local_rows, local_cols = front.shape
    tile_rows = local_rows // TB
    tile_cols = local_cols // TB
    grid = tile_cols * col_count
    held = child_tiles.shape[0]
    capacity = 2 * max(1, (held + devices - 1) // devices)
    row_index = lax.axis_index("row")
    col_index = lax.axis_index("col")
    device = row_index * col_count + col_index
    half = TB // 2

    homes = (PD + local_rows - 1) // local_rows
    most = max(1, homes * capacity // 2)
    picked = pick(tile_target, tile_count, child_tiles, most, grid)
    inner, pair = min(2, row_count) * col_count, min(2, col_count)
    gathered = jnp.concatenate(collect(picked, devices, inner, pair), axis=0)
    gathered, tile_target = lax.optimization_barrier((gathered, tile_target))
    outgoing = stage(tile_target, tile_count, child_tiles, devices, capacity, grid, tile_rows, tile_cols, col_count)
    gathered = jnp.concatenate(collect_last(gathered, inner, pair), axis=0)
    gathered, outgoing = lax.optimization_barrier((gathered, outgoing))
    label = gathered.reshape(devices, -1, LANES)[:, most * half, :most].astype(jnp.int32).reshape(-1)
    corner = front
    if homes > 1:
        corner = [front[:, :PD]] + [lax.ppermute(front[:, :PD], "row", [(home, 0)]) for home in range(1, homes)]
        corner = jnp.concatenate(corner, axis=0)

    incoming = lax.all_to_all(
        outgoing.reshape(devices, capacity * half + 8, LANES), AXES, split_axis=0, concat_axis=0, tiled=True
    )

    packed = inverse_of_factor(label, device.reshape(1), corner, gathered, most, devices)
    order = masks(devices)
    order = order[:1] + [m for m in order[1:] if m >= col_count] + [m for m in order[1:] if m < col_count]
    part = scatter(packed, AXES, device, order, devices)
    part, incoming = lax.optimization_barrier((part, incoming))
    first = jnp.clip(PD - col_index * local_cols, 0, local_cols).reshape(1)
    landing = incoming[:, capacity * half, :capacity].astype(jnp.int32).reshape(-1)
    product, *panel = assemble(
        landing, first, front, incoming.reshape(-1, LANES), probe, capacity, tile_rows, tile_cols, bits_reversed(col_count)
    )

    share = product.reshape(-1, product.shape[2])
    order = order[::-1]
    sums = masks(col_count)
    panel_order = sums[::-1]
    far = [(0, panel_order[0])]
    sent = [lax.ppermute(panel[0], "col", far)]
    for mask in sums[:-1]:
        share = halve(share, "col", col_index, mask, col_count)
    part = double(part, AXES, device, order[0], devices)
    share, part, *panel[1:] = lax.optimization_barrier((share, part, *panel[1:]))
    sent += [lax.ppermute(piece, "col", far) for piece in panel[1:MIDDLE]]
    share = halve(share, "col", col_index, sums[-1], col_count)
    for mask in order[1:-2]:
        part = double(part, AXES, device, mask, devices)
    share, part, *panel[MIDDLE:] = lax.optimization_barrier((share, part, *panel[MIDDLE:]))
    sent += [lax.ppermute(piece, "col", far) for piece in panel[MIDDLE:]]
    part = double(part, AXES, device, order[-2], devices)
    held = {0: panel, panel_order[0]: sent}

    top_order = masks(row_count)[::-1]
    if homes == 1:
        top = spread(share[:PD], "row", row_index, top_order[:1], row_count)
        part = double(part, AXES, device, order[-1], devices)
        top = spread(top, "row", row_index, top_order[1:], row_count)
    else:
        pieces = []
        for home in range(homes):
            rows = min(PD - home * local_rows, local_rows)
            pieces.append(jnp.where(row_index == home, share[:rows], 0.0))
        top = all_sum(jnp.concatenate(pieces, axis=0), "row", row_index, masks(row_count), row_count)
        part = double(part, AXES, device, order[-1], devices)
    inverse = unpack(part)

    for mask in panel_order:
        for d in range(0, col_count, 2 * mask):
            if d + mask not in held:
                held[d + mask] = [lax.ppermute(piece, "col", [(d, d + mask)]) for piece in held[d]]
    panels = [held[d] for d in range(col_count)]

    dot = functools.partial(jnp.dot, precision=lax.Precision.HIGH, preferred_element_type=jnp.float32)
    weights = lax.dot_general(
        inverse, dot(inverse, top), (((0,), (0,)), ((), ())), precision=lax.Precision.HIGH, preferred_element_type=jnp.float32
    )
    width = PD // col_count
    mine = lax.dynamic_slice_in_dim(inverse, col_index * width, width, 0)
    return finish(jnp.stack([col_index, row_index * local_rows]), panels, mine, weights, share)


def solution(mesh):
    return jax.shard_map(
        per_device,
        mesh=mesh,
        in_specs=(
            P("row", "col"),
            P(("row", "col"), None),
            P(("row", "col")),
            P(("row", "col")),
            P("col", None),
        ),
        out_specs=(P("row", "col"), P("row", "col")),
        check_vma=False,
    )
```

```python
import functools

import jax
import jax.numpy as jnp
import numpy as np
from jax import lax
from jax.experimental import pallas as pl
from jax.experimental.pallas import tpu as pltpu
from jax.sharding import PartitionSpec as P

NB = 512
PANELS = 2
PD = NB * PANELS
TB = 64
SLOTS = 32
LANES = 128
NBLK = PD // LANES
PACKED = NBLK * (NBLK + 1) // 2
AXES = ("row", "col")
HIGH = lax.Precision.HIGHEST
MIB = 1 << 20
MIDDLE = 3
PIECES = 4


def block_index(r, c):
    return r * (r + 1) // 2 + c


def left_half(shape):
    return lax.broadcasted_iota(jnp.int32, shape, len(shape) - 1) < TB


def magic(divisor, limit):
    x = np.arange(limit, dtype=np.int64)
    for shift in range(8, 31):
        m = (1 << shift) // divisor + 1
        if m * limit < 1 << 31 and np.array_equal((x * m) >> shift, x // divisor):
            return m, shift
    raise ValueError("no multiplier")


def quotient(x, divisor, limit):
    m, shift = magic(divisor, limit)
    return (x * m) >> shift


def is_live(count_ref, t):
    return t % SLOTS < count_ref[t // SLOTS]


def pick_kernel(
    held, most, grid,
    target_ref, count_ref,
    tiles_ref,
    out_ref,
    flat_ref, pair_ref, label_ref, filled_ref,
):
    half = TB // 2
    side = PD // TB
    filled_ref[0] = 0
    for s in range(most):
        label_ref[s] = -1

    def look(t, carry):
        r = quotient(target_ref[t], grid, grid * grid)
        c = target_ref[t] - r * grid

        @pl.when(is_live(count_ref, t) & (r < side) & (c < side))
        def _():
            left = left_half((half, LANES))
            group = tiles_ref[pl.ds(pl.multiple_of(t // 8 * 8, 8), 8), :]
            row = lax.broadcasted_iota(jnp.int32, group.shape, 0)
            line = jnp.sum(jnp.where(row == t % 8, group, 0.0), axis=0, keepdims=True)
            for k in range(half):
                flat_ref[k : k + 1, :] = line[:, k * LANES : (k + 1) * LANES]
            flat = flat_ref[...]
            turned = pltpu.roll(flat, TB, 1)
            pair_ref[pl.ds(0, half, stride=2), :] = jnp.where(left, flat, turned)
            pair_ref[pl.ds(1, half, stride=2), :] = jnp.where(left, turned, flat)
            natural = pair_ref[...]
            mirrored = natural.T[:TB]
            mirrored = jnp.concatenate([mirrored, mirrored], axis=1)
            swap = r // 2 > c // 2
            value = jnp.where(swap, mirrored, natural) * jnp.where(r // 2 == c // 2, 2.0, 1.0)
            filled = filled_ref[0]
            out_ref[pl.ds(pl.multiple_of(filled * half, half), half), :] = jnp.where(left, value[:half], pltpu.roll(value[half:], TB, 1))
            label_ref[filled] = jnp.where(swap, c * side + r, r * side + c)
            filled_ref[0] = filled + 1

        return carry

    lax.fori_loop(0, held, look, 0, unroll=4)
    lane = lax.broadcasted_iota(jnp.int32, (8, LANES), 1)
    line = jnp.full((8, LANES), -1, jnp.int32)
    for s in range(most):
        line = jnp.where(lane == s, label_ref[s], line)
    out_ref[most * half : most * half + 8, :] = line.astype(jnp.float32)


def pick(target, count, child_tiles, most, grid):
    held = child_tiles.shape[0]
    smem = pl.BlockSpec(memory_space=pltpu.SMEM)
    rows = most * TB // 2 + 8
    return pl.pallas_call(
        functools.partial(pick_kernel, held, most, grid),
        grid=(1,),
        out_shape=jax.ShapeDtypeStruct((rows, LANES), jnp.float32),
        in_specs=[smem] * 2 + [pl.BlockSpec((held, TB * TB), lambda i: (0, 0))],
        out_specs=pl.BlockSpec((rows, LANES), lambda i: (0, 0)),
        scratch_shapes=[
            pltpu.VMEM((TB // 2, LANES), jnp.float32),
            pltpu.VMEM((TB, LANES), jnp.float32),
            pltpu.SMEM((most,), jnp.int32),
            pltpu.SMEM((1,), jnp.int32),
        ],
        compiler_params=pltpu.CompilerParams(vmem_limit_bytes=16 * MIB),
        name="pick",
    )(target, count, child_tiles)


def stage_kernel(
    held, devices, capacity, grid, tile_rows, tile_cols, col_count,
    target_ref, tally_ref,
    tiles_ref,
    out_ref,
    flat_ref, pair_ref, count_ref, slot_ref, landing_ref,
):
    half = TB // 2
    for d in range(devices):
        count_ref[d] = 0

    def clear(s, carry):
        landing_ref[s] = -1
        return carry

    lax.fori_loop(0, devices * capacity, clear, 0)

    def spread_out(g, carry):
        rows = tiles_ref[pl.ds(pl.multiple_of(g * 8, 8), 8), :]
        for k in range(half):
            flat_ref[pl.ds(g * 8 * half + k, 8, stride=half), :] = rows[:, k * LANES : (k + 1) * LANES]
        return carry

    lax.fori_loop(0, held // 8, spread_out, 0, unroll=2)

    def assign(t, carry):
        alive = is_live(tally_ref, t)
        r = quotient(target_ref[t], grid, grid * grid)
        c = target_ref[t] - r * grid
        for m, (a, b) in enumerate(((r, c), (c, r))):
            home = quotient(a, tile_rows, grid)
            side = quotient(b, tile_cols, grid)
            owner = home * col_count + side
            place = (a - home * tile_rows) * tile_cols + (b - side * tile_cols)
            filled = count_ref[owner]
            count_ref[owner] = filled + 1
            slot = owner * capacity + filled
            slot_ref[m * held + t] = owner * (capacity * half + 8) + filled * half
            landing_ref[slot] = jnp.where(alive, place, -1)
        return carry

    lax.fori_loop(0, held, assign, 0, unroll=4)

    def put(index, value):
        out_ref[pl.ds(pl.multiple_of(slot_ref[index], 8), half), :] = value

    def quad(q, carry):
        left = left_half((half, LANES))
        naturals = []
        for p in range(2):
            a = flat_ref[pl.ds(pl.multiple_of((4 * q + 2 * p) * half, half), half), :]
            b = flat_ref[pl.ds(pl.multiple_of((4 * q + 2 * p + 1) * half, half), half), :]
            pair_ref[p, pl.ds(0, half, stride=2), :] = jnp.where(left, a, pltpu.roll(b, TB, 1))
            pair_ref[p, pl.ds(1, half, stride=2), :] = jnp.where(left, pltpu.roll(a, TB, 1), b)
            naturals.append(pair_ref[p, :, :])
        turned = jnp.concatenate(naturals, axis=0).T
        for m, values, order in (
            (0, naturals[0], (0, 1)),
            (0, naturals[1], (2, 3)),
            (1, turned[:TB], (0, 2)),
            (1, turned[TB:], (1, 3)),
        ):
            up, low = values[:half], values[half:]
            put(m * held + 4 * q + order[0], jnp.where(left, up, pltpu.roll(low, TB, 1)))
            put(m * held + 4 * q + order[1], jnp.where(left, pltpu.roll(up, TB, 1), low))
        return carry

    lax.fori_loop(0, held // 4, quad, 0, unroll=4)

    lane = lax.broadcasted_iota(jnp.int32, (8, LANES), 1)

    def label(d, carry):
        line = jnp.full((8, LANES), -1, jnp.int32)
        for s in range(capacity):
            line = jnp.where(lane == s, landing_ref[d * capacity + s], line)
        at = d * (capacity * half + 8) + capacity * half
        out_ref[pl.ds(pl.multiple_of(at, 8), 8), :] = line.astype(jnp.float32)
        return carry

    lax.fori_loop(0, devices, label, 0)


def stage(target, tally, child_tiles, devices, capacity, grid, tile_rows, tile_cols, col_count):
    held = child_tiles.shape[0]
    half = TB // 2
    smem = pl.BlockSpec(memory_space=pltpu.SMEM)
    rows = devices * (capacity * half + 8)
    return pl.pallas_call(
        functools.partial(stage_kernel, held, devices, capacity, grid, tile_rows, tile_cols, col_count),
        grid=(1,),
        out_shape=jax.ShapeDtypeStruct((rows, LANES), jnp.float32),
        in_specs=[smem] * 2 + [pl.BlockSpec((held, TB * TB), lambda i: (0, 0))],
        out_specs=pl.BlockSpec((rows, LANES), lambda i: (0, 0)),
        scratch_shapes=[
            pltpu.VMEM((held * half, LANES), jnp.float32),
            pltpu.VMEM((2, TB, LANES), jnp.float32),
            pltpu.SMEM((devices,), jnp.int32),
            pltpu.SMEM((2 * held,), jnp.int32),
            pltpu.SMEM((devices * capacity,), jnp.int32),
        ],
        compiler_params=pltpu.CompilerParams(vmem_limit_bytes=24 * MIB),
        name="stage",
    )(target, tally, child_tiles)


def split(x):
    high = x.astype(jnp.bfloat16)
    return high, (x - high.astype(jnp.float32)).astype(jnp.bfloat16)


def dot3(left_high, left_low, right_high, right_low):
    dot = functools.partial(jnp.dot, preferred_element_type=jnp.float32)
    return dot(left_high, right_high) + (dot(left_high, right_low) + dot(left_low, right_high))


def lane_splat(x, lane):
    return jnp.broadcast_to(x[:, lane : lane + 1], x.shape)


def row_splat(ref, row):
    return jnp.broadcast_to(ref[row : row + 1, :], (8, LANES))


def inverse_factor(strips, splat_ref):
    strips = list(strips)
    lane = lax.broadcasted_iota(jnp.int32, (8, LANES), 1)
    sub = lax.broadcasted_iota(jnp.int32, (8, LANES), 0)
    result = []
    for k in range(LANES // 8):
        strip = strips[k]
        columns = [lane_splat(strip, 8 * k + t) for t in range(8)]
        for t in range(8):
            splat_ref[8 * t : 8 * t + 8, :] = columns[t]
        e = [[row_splat(splat_ref, 8 * t + s) if s <= t else None for t in range(8)] for s in range(8)]
        low = [[None] * 8 for _ in range(8)]
        inv = [None] * 8
        for s in range(8):
            inv[s] = lax.rsqrt(e[s][s])
            for t in range(s + 1, 8):
                low[t][s] = e[s][t] * inv[s]
            for t in range(s + 1, 8):
                for u in range(t, 8):
                    e[t][u] = e[t][u] - low[t][s] * low[u][s]
        li = [[None] * 8 for _ in range(8)]
        for s in range(8):
            li[s][s] = inv[s]
            for r in range(s + 1, 8):
                total = low[r][s] * li[s][s]
                for q in range(s + 1, r):
                    total = total + low[r][q] * li[q][s]
                li[r][s] = -inv[r] * total
        inside = (lane >= 8 * k) & (lane < 8 * k + 8)
        unit = jnp.where(lane - 8 * k == sub, 1.0, 0.0)
        strip = jnp.where(inside, unit, strip)
        splat_ref[64:72, :] = strip
        rows = [row_splat(splat_ref, 64 + s) for s in range(8)]
        u = []
        for r in range(8):
            total = li[r][0] * rows[0]
            for s in range(1, r + 1):
                total = total + li[r][s] * rows[s]
            u.append(total)
        mine = u[0]
        for r in range(1, 8):
            mine = jnp.where(sub == r, u[r], mine)
        result.append(jnp.where(lane < 8 * k + 8, mine, 0.0))
        if k + 1 == LANES // 8:
            break
        v = []
        for s in range(8):
            total = li[s][s] * u[s]
            for r in range(s + 1, 8):
                total = total + li[r][s] * u[r]
            v.append(total)
        for i in range(k + 1, LANES // 8):
            old = strips[i]
            total = lane_splat(old, 8 * k) * v[0]
            for s in range(1, 8):
                total = total + lane_splat(old, 8 * k + s) * v[s]
            strips[i] = jnp.where(inside, 0.0, old) - total
    return result


def factor_kernel(
    most, senders,
    label_ref, me_ref,
    front_ref, tiles_ref,
    packed_ref,
    out_ref, top_ref, small_ref, high_ref, low_ref, splat_ref, semaphore,
):
    @pl.when(me_ref[0] == 0)
    def _():
        copy = pltpu.make_async_copy(front_ref.at[:PD, :PD], out_ref, semaphore)
        copy.start()
        copy.wait()
        factor(most, senders, label_ref, front_ref, tiles_ref, packed_ref, out_ref, top_ref, small_ref, high_ref, low_ref, splat_ref)


def factor(most, senders, label_ref, front_ref, tiles_ref, packed_ref, out_ref, top_ref, small_ref, high_ref, low_ref, splat_ref):
    half = TB // 2
    side = PD // TB
    for r in range(NBLK):
        rows = slice(r * LANES, (r + 1) * LANES)
        if r > 0:
            out_ref[rows, : r * LANES] = jnp.zeros((LANES, r * LANES), jnp.float32)
    left = left_half((half, LANES))
    group = 8 if most * senders % 8 == 0 else 2

    def place(g, carry):
        parts = []
        for e in range(group):
            s = g * group + e
            p = label_ref[s]
            alive = p >= 0
            p = jnp.clip(p, 0, side * side - 1)
            r, c = p // side, p % side
            even = c % 2 == 0
            source = s // most * (most * half + 8) + s % most * half
            packed = tiles_ref[pl.ds(pl.multiple_of(source, 8), half), :]
            turned = pltpu.roll(packed, TB, 1)
            mask = (left == even) & alive
            top = jnp.where(mask, jnp.where(even, packed, turned), 0.0)
            low = jnp.where(mask, jnp.where(even, turned, packed), 0.0)
            parts.append((r, c // 2, top, low))
        for r, c, top, low in parts:
            cols = pl.ds(pl.multiple_of(c * LANES, LANES), LANES)
            out_ref[pl.ds(pl.multiple_of(r * TB, TB), half), cols] += top
            out_ref[pl.ds(pl.multiple_of(r * TB + half, half), half), cols] += low
        return carry

    lax.fori_loop(0, most * senders // group, place, 0)

    eye = jnp.where(
        lax.broadcasted_iota(jnp.int32, (LANES, LANES), 0) == lax.broadcasted_iota(jnp.int32, (LANES, LANES), 1), 1.0, 0.0
    )

    def outer(k, carry):
        at = pl.multiple_of(k * LANES, LANES)
        here = pl.ds(at, LANES)
        block = out_ref[here, here]
        block = 0.5 * (block + block.T)
        small_ref[...] = block
        strips = inverse_factor([small_ref[8 * i : 8 * i + 8, :] for i in range(LANES // 8)], splat_ref)
        for i, strip in enumerate(strips):
            small_ref[8 * i : 8 * i + 8, :] = strip
        out_ref[here, here] = eye
        top = dot3(*split(small_ref[...]), *split(out_ref[here, :]))
        top_ref[...] = top
        column = lax.broadcasted_iota(jnp.int32, (LANES, PD), 1)
        out_ref[here, :] = jnp.where(column < at + LANES, top, 0.0)
        high_ref[...], low_ref[...] = split(top)
        for step in range(NBLK - 1):

            @pl.when(k == step)
            def _():
                edge = (step + 1) * LANES
                for start in range(edge, PD, LANES):
                    there = slice(start, start + LANES)
                    across = split(top_ref[:, there].T)
                    out_ref[there, :edge] = jnp.where(
                        lax.broadcasted_iota(jnp.int32, (LANES, edge), 1) < edge - LANES, out_ref[there, :edge], 0.0
                    ) - dot3(*across, high_ref[:, :edge], low_ref[:, :edge])
                    out_ref[there, start:] -= dot3(*across, high_ref[:, start:], low_ref[:, start:])

        return carry

    lax.fori_loop(0, NBLK, outer, 0)
    for r in range(NBLK):
        for c in range(r + 1):
            base = block_index(r, c) * LANES
            packed_ref[base : base + LANES, :] = out_ref[r * LANES : (r + 1) * LANES, c * LANES : (c + 1) * LANES]


def inverse_of_factor(label, me, front, tiles, most, senders):
    smem = pl.BlockSpec(memory_space=pltpu.SMEM)
    return pl.pallas_call(
        functools.partial(factor_kernel, most, senders),
        grid=(1,),
        out_shape=jax.ShapeDtypeStruct((PACKED * LANES, LANES), jnp.float32),
        in_specs=[smem, smem, pl.BlockSpec(memory_space=pl.ANY), pl.BlockSpec(tiles.shape, lambda i: (0, 0))],
        out_specs=pl.BlockSpec((PACKED * LANES, LANES), lambda i: (0, 0)),
        scratch_shapes=[
            pltpu.VMEM((PD, PD), jnp.float32),
            pltpu.VMEM((LANES, PD), jnp.float32),
            pltpu.VMEM((LANES, LANES), jnp.float32),
            pltpu.VMEM((LANES, PD), jnp.bfloat16),
            pltpu.VMEM((LANES, PD), jnp.bfloat16),
            pltpu.VMEM((72, LANES), jnp.float32),
            pltpu.SemaphoreType.DMA,
        ],
        compiler_params=pltpu.CompilerParams(vmem_limit_bytes=56 * MIB),
        name="factor",
    )(label, me, front, tiles)


def unpack_kernel(packed_ref, out_ref):
    for r in range(NBLK):
        for c in range(NBLK):
            rows, cols = slice(r * LANES, (r + 1) * LANES), slice(c * LANES, (c + 1) * LANES)
            if c > r:
                out_ref[rows, cols] = jnp.zeros((LANES, LANES), jnp.float32)
            else:
                base = block_index(r, c) * LANES
                out_ref[rows, cols] = packed_ref[base : base + LANES, :]


def unpack(packed):
    vmem = pl.BlockSpec(memory_space=pltpu.VMEM)
    return pl.pallas_call(
        unpack_kernel,
        out_shape=jax.ShapeDtypeStruct((PD, PD), jnp.float32),
        in_specs=[vmem],
        out_specs=vmem,
        compiler_params=pltpu.CompilerParams(vmem_limit_bytes=16 * MIB),
        name="unpack",
    )(packed)


def assemble_kernel(
    slots, capacity, tile_cols, limit, row_chunk, width, order,
    landing_ref, first_ref,
    front_ref, incoming_ref, probe_ref,
    product_ref, *rest,
):
    panels, (matrix_ref, high_ref, low_ref, semaphore) = rest[:-4], rest[-4:]
    copy = pltpu.make_async_copy(front_ref, matrix_ref, semaphore)
    copy.start()
    step = 256 if probe_ref.shape[0] % 256 == 0 else 128
    half = TB // 2

    def cut(s, carry):
        rows = pl.ds(pl.multiple_of(s * step, step), step)
        index = lax.broadcasted_iota(jnp.int32, (step, probe_ref.shape[1]), 0) + s * step
        high, low = split(jnp.where(index >= first_ref[0], probe_ref[rows, :], 0.0))
        high_ref[rows, :] = high
        low_ref[rows, :] = low
        return carry

    lax.fori_loop(0, probe_ref.shape[0] // step, cut, 0)
    copy.wait()
    block = capacity * half + 8
    group = 16 if slots % 16 == 0 else 2
    left = left_half((half, LANES))

    def place(g, carry):
        parts = []
        for e in range(group):
            s = g * group + e
            p = landing_ref[s]
            alive = p >= 0
            p = jnp.maximum(p, 0)
            r = quotient(p, tile_cols, limit)
            c = p - r * tile_cols
            even = c % 2 == 0
            source = s // capacity * block + s % capacity * half
            packed = incoming_ref[pl.ds(pl.multiple_of(source, 8), half), :]
            turned = pltpu.roll(packed, TB, 1)
            mask = (left == even) & alive
            top = jnp.where(mask, jnp.where(even, packed, turned), 0.0)
            low = jnp.where(mask, jnp.where(even, turned, packed), 0.0)
            parts.append((r, c // 2, top, low))
        for r, c, top, low in parts:
            cols = pl.ds(pl.multiple_of(c * LANES, LANES), LANES)
            matrix_ref[pl.ds(pl.multiple_of(r * TB, TB), half), cols] += top
            matrix_ref[pl.ds(pl.multiple_of(r * TB + half, half), half), cols] += low
        return carry

    lax.fori_loop(0, slots // group, place, 0)
    rows = matrix_ref.shape[0] // len(panels)
    for i, panel_ref in enumerate(panels):
        panel_ref[...] = matrix_ref[i * rows : (i + 1) * rows, :PD]

    def multiply(b, carry):
        rows = pl.ds(pl.multiple_of(b * row_chunk, row_chunk), row_chunk)
        high, low = split(matrix_ref[rows, :])
        dot = functools.partial(jnp.dot, preferred_element_type=jnp.float32)
        total = dot(high, high_ref[...]) + (dot(high, low_ref[...]) + dot(low, high_ref[...]))
        for j, at in enumerate(order):
            product_ref[at, rows, :] = total[:, j * width : (j + 1) * width]
        return carry

    lax.fori_loop(0, matrix_ref.shape[0] // row_chunk, multiply, 0)


def assemble(landing, first, front, incoming, probe, capacity, tile_rows, tile_cols, order):
    local_rows, local_cols = front.shape
    columns = probe.shape[1]
    width = columns // len(order)
    smem = pl.BlockSpec(memory_space=pltpu.SMEM)
    vmem = pl.BlockSpec(memory_space=pltpu.VMEM)
    row_chunk = next(n for n in (384, 192, 64) if local_rows % n == 0)
    return pl.pallas_call(
        functools.partial(
            assemble_kernel, landing.shape[0], capacity, tile_cols, tile_rows * tile_cols, row_chunk, width, order
        ),
        out_shape=(jax.ShapeDtypeStruct((len(order), local_rows, width), jnp.float32),)
        + (jax.ShapeDtypeStruct((local_rows // PIECES, PD), jnp.float32),) * PIECES,
        in_specs=[smem] * 2 + [pl.BlockSpec(memory_space=pl.ANY), vmem, vmem],
        out_specs=(vmem,) * (1 + PIECES),
        scratch_shapes=[
            pltpu.VMEM((local_rows, local_cols), jnp.float32),
            pltpu.VMEM((local_cols, columns), jnp.bfloat16),
            pltpu.VMEM((local_cols, columns), jnp.bfloat16),
            pltpu.SemaphoreType.DMA,
        ],
        compiler_params=pltpu.CompilerParams(vmem_limit_bytes=56 * MIB),
        name="assemble",
    )(landing, first, front, incoming, probe)


def finish_kernel(
    sources, width,
    where_ref, *refs,
):
    panels = refs[: sources * PIECES]
    inverse_ref, weights_ref, share_ref, solved_ref, sketch_ref, panel_ref, semaphore = refs[sources * PIECES :]
    col, row_start = where_ref[0], where_ref[1]
    piece = panel_ref.shape[0] // PIECES
    for j in range(sources):

        @pl.when(col == j)
        def _():
            moves = [
                pltpu.make_async_copy(panels[j * PIECES + i], panel_ref.at[i * piece : (i + 1) * piece], semaphore.at[i])
                for i in range(PIECES)
            ]
            for move in moves:
                move.start()
            for move in moves:
                move.wait()

    right_high, right_low = split(jnp.concatenate([inverse_ref[...].T, weights_ref[...]], axis=1))
    dot = functools.partial(jnp.dot, preferred_element_type=jnp.float32)
    step = next(n for n in (384, 192, 64) if panel_ref.shape[0] % n == 0)

    def body(b, carry):
        rows = pl.ds(pl.multiple_of(b * step, step), step)
        high, low = split(panel_ref[rows, :])
        total = dot(high, right_high) + (dot(high, right_low) + dot(low, right_high))
        index = row_start + b * step + lax.broadcasted_iota(jnp.int32, (step, width), 0)
        column = col * width + lax.broadcasted_iota(jnp.int32, (step, width), 1)
        solved_ref[rows, :] = jnp.where(index >= (column // NB) * NB, total[:, :width], 0.0)
        rest = share_ref[rows, :] - total[:, width:]
        index = row_start + b * step + lax.broadcasted_iota(jnp.int32, rest.shape, 0)
        sketch_ref[rows, :] = jnp.where(index >= PD, rest, 0.0)
        return carry

    lax.fori_loop(0, panel_ref.shape[0] // step, body, 0)


def finish(where, panels, inverse, weights, share):
    local_rows = share.shape[0]
    width = inverse.shape[0]
    vmem = pl.BlockSpec(memory_space=pltpu.VMEM)
    return pl.pallas_call(
        functools.partial(finish_kernel, len(panels), width),
        out_shape=(
            jax.ShapeDtypeStruct((local_rows, width), jnp.float32),
            jax.ShapeDtypeStruct(share.shape, jnp.float32),
        ),
        in_specs=[pl.BlockSpec(memory_space=pltpu.SMEM)] + [pl.BlockSpec(memory_space=pl.ANY)] * (len(panels) * PIECES) + [vmem] * 3,
        out_specs=(vmem, vmem),
        scratch_shapes=[pltpu.VMEM((local_rows, PD), jnp.float32), pltpu.SemaphoreType.DMA((PIECES,))],
        compiler_params=pltpu.CompilerParams(vmem_limit_bytes=28 * MIB),
        name="finish",
    )(where, *sum(panels, []), inverse, weights, share)


def masks(count):
    return [1 << b for b in range(count.bit_length() - 1)]


def exchange(x, axis, mask, count):
    return lax.ppermute(x, axis, [(d, d ^ mask) for d in range(count)])


def choose(bit, x):
    h = x.shape[0] // 2
    return jnp.where(bit, x[h:], x[:h]), jnp.where(bit, x[:h], x[h:])


def halve(x, axis, index, mask, count):
    keep, send = choose((index & mask) != 0, x)
    return keep + exchange(send, axis, mask, count)


def double(x, axis, index, mask, count):
    other = exchange(x, axis, mask, count)
    bit = (index & mask) != 0
    return jnp.concatenate([jnp.where(bit, other, x), jnp.where(bit, x, other)], axis=0)


def all_sum(x, axis, index, order, count):
    for mask in order:
        x = halve(x, axis, index, mask, count)
    for mask in order[::-1]:
        x = double(x, axis, index, mask, count)
    return x


def spread(x, axis, index, order, count):
    for mask in order:
        other = lax.ppermute(x, axis, [(d, d + mask) for d in range(0, count, 2 * mask)])
        x = jnp.where((index & (2 * mask - 1)) == mask, other, x)
    return x


def collect(x, count, inner, pair):
    heads = range(0, inner, pair)
    offsets = [far + near for far in range(0, count, inner) for near in range(pair) if far + near > 0]
    return [x] + [lax.ppermute(x, AXES, [(e + offset, e) for e in heads]) for offset in offsets]


def collect_last(x, inner, pair):
    return [x] + [lax.ppermute(x, AXES, [(e, 0)]) for e in range(pair, inner, pair)]


def scatter(x, axis, index, order, count):
    done = 0
    for mask in order:
        pairs = [(d, d + mask) for d in range(count) if d & done == d]
        h = x.shape[0] // 2
        x = jnp.where((index & mask) != 0, lax.ppermute(x[h:], axis, pairs), x[:h])
        done |= mask
    return x


def bits_reversed(count):
    width = count.bit_length() - 1
    return [sum(((j >> b) & 1) << (width - 1 - b) for b in range(width)) for j in range(count)]


def per_device(front, child_tiles, tile_target, tile_count, probe):
    row_count = lax.axis_size("row")
    col_count = lax.axis_size("col")
    devices = row_count * col_count
    local_rows, local_cols = front.shape
    tile_rows = local_rows // TB
    tile_cols = local_cols // TB
    grid = tile_cols * col_count
    held = child_tiles.shape[0]
    capacity = 2 * max(1, (held + devices - 1) // devices)
    row_index = lax.axis_index("row")
    col_index = lax.axis_index("col")
    device = row_index * col_count + col_index
    half = TB // 2

    homes = (PD + local_rows - 1) // local_rows
    most = max(1, homes * capacity // 2)
    picked = pick(tile_target, tile_count, child_tiles, most, grid)
    inner, pair = min(2, row_count) * col_count, min(2, col_count)
    gathered = jnp.concatenate(collect(picked, devices, inner, pair), axis=0)
    gathered, tile_target = lax.optimization_barrier((gathered, tile_target))
    outgoing = stage(tile_target, tile_count, child_tiles, devices, capacity, grid, tile_rows, tile_cols, col_count)
    gathered = jnp.concatenate(collect_last(gathered, inner, pair), axis=0)
    gathered, outgoing = lax.optimization_barrier((gathered, outgoing))
    label = gathered.reshape(devices, -1, LANES)[:, most * half, :most].astype(jnp.int32).reshape(-1)
    corner = front
    if homes > 1:
        corner = [front[:, :PD]] + [lax.ppermute(front[:, :PD], "row", [(home, 0)]) for home in range(1, homes)]
        corner = jnp.concatenate(corner, axis=0)

    incoming = lax.all_to_all(
        outgoing.reshape(devices, capacity * half + 8, LANES), AXES, split_axis=0, concat_axis=0, tiled=True
    )

    packed = inverse_of_factor(label, device.reshape(1), corner, gathered, most, devices)
    order = masks(devices)
    order = order[:1] + [m for m in order[1:] if m >= col_count] + [m for m in order[1:] if m < col_count]
    part = scatter(packed, AXES, device, order, devices)
    part, incoming = lax.optimization_barrier((part, incoming))
    first = jnp.clip(PD - col_index * local_cols, 0, local_cols).reshape(1)
    landing = incoming[:, capacity * half, :capacity].astype(jnp.int32).reshape(-1)
    product, *panel = assemble(
        landing, first, front, incoming.reshape(-1, LANES), probe, capacity, tile_rows, tile_cols, bits_reversed(col_count)
    )

    share = product.reshape(-1, product.shape[2])
    order = order[::-1]
    sums = masks(col_count)
    panel_order = sums[::-1]
    far = [(0, panel_order[0])]
    sent = [lax.ppermute(panel[0], "col", far)]
    for mask in sums[:-1]:
        share = halve(share, "col", col_index, mask, col_count)
    part = double(part, AXES, device, order[0], devices)
    share, part, *panel[1:] = lax.optimization_barrier((share, part, *panel[1:]))
    sent += [lax.ppermute(piece, "col", far) for piece in panel[1:MIDDLE]]
    share = halve(share, "col", col_index, sums[-1], col_count)
    for mask in order[1:-2]:
        part = double(part, AXES, device, mask, devices)
    share, part, *panel[MIDDLE:] = lax.optimization_barrier((share, part, *panel[MIDDLE:]))
    sent += [lax.ppermute(piece, "col", far) for piece in panel[MIDDLE:]]
    part = double(part, AXES, device, order[-2], devices)
    held = {0: panel, panel_order[0]: sent}

    top_order = masks(row_count)[::-1]
    if homes == 1:
        top = spread(share[:PD], "row", row_index, top_order[:1], row_count)
        part = double(part, AXES, device, order[-1], devices)
        top = spread(top, "row", row_index, top_order[1:], row_count)
    else:
        pieces = []
        for home in range(homes):
            rows = min(PD - home * local_rows, local_rows)
            pieces.append(jnp.where(row_index == home, share[:rows], 0.0))
        top = all_sum(jnp.concatenate(pieces, axis=0), "row", row_index, masks(row_count), row_count)
        part = double(part, AXES, device, order[-1], devices)
    inverse = unpack(part)

    for mask in panel_order:
        for d in range(0, col_count, 2 * mask):
            if d + mask not in held:
                held[d + mask] = [lax.ppermute(piece, "col", [(d, d + mask)]) for piece in held[d]]
    panels = [held[d] for d in range(col_count)]

    dot = functools.partial(jnp.dot, precision=lax.Precision.HIGH, preferred_element_type=jnp.float32)
    weights = lax.dot_general(
        inverse, dot(inverse, top), (((0,), (0,)), ((), ())), precision=lax.Precision.HIGH, preferred_element_type=jnp.float32
    )
    width = PD // col_count
    mine = lax.dynamic_slice_in_dim(inverse, col_index * width, width, 0)
    return finish(jnp.stack([col_index, row_index * local_rows]), panels, mine, weights, share)


def solution(mesh):
    return jax.shard_map(
        per_device,
        mesh=mesh,
        in_specs=(
            P("row", "col"),
            P(("row", "col"), None),
            P(("row", "col")),
            P(("row", "col")),
            P("col", None),
        ),
        out_specs=(P("row", "col"), P("row", "col")),
        check_vma=False,
    )
```
